32 devices in a mesh: dp: 4 (over z), seq: 8 (over y, x, core).
Axes of the slice: x: 2, y: 2, z: 4, core: 2. Of those that a mesh axis runs over, the one named last changes fastest.
Arguments:
- tokens: bfloat16 [4, 2048, 2048], P('dp', 'seq'), may hold values from -6 to 6
- cotangent: bfloat16 [4, 2048, 2048], P('dp', 'seq'), may hold values from -6 to 6
- kernel: bfloat16 [2048, 2048], P('seq'), may hold values from -6 to 6
- first_factor: bfloat16 [8, 256, 256], P('seq'), may hold values from -0.375 to 0.375
- second_factor: bfloat16 [256, 8, 8], P('seq'), may hold values from -2 to 2
Outputs:
- grad_kernel: bfloat16 [2048, 2048], P('seq')
- grad_first: float32 [8, 256, 256], P('seq')
- grad_second: float32 [256, 8, 8], P('seq')
The draws below stay inside these ranges and needn't reach their ends.
All inputs are finite; a program needn't handle non-finite values.
Results may differ from the reference program's by a relative error of at most 0.0058.
Values may be sent and summed in bfloat16 or wider, within the bound.
A program may use at most 64 MiB of HBM per device.

```python
import math
import jax
import jax.numpy as jnp
from jax import lax

D = 2048
GB = 256
SEQS = 4
L = 2048
GA = 8


def levels(rng, extent, cuts, smallest, largest):
    gain = 1.0
    for dim, blocks in cuts:
        heights = jax.random.uniform(jax.random.fold_in(jax.random.fold_in(rng, 6), dim), (blocks,), jnp.float32, smallest / len(cuts), largest / len(cuts))
        gain = gain * jnp.repeat(jnp.exp(heights), extent[dim] // blocks).reshape((-1,) + (1,) * (len(extent) - 1 - dim))
    return gain


def normal_values(stream_key, dims, scale, bound, pieces=(), held_as=jnp.bfloat16):
    entries = scale * jax.random.normal(stream_key, dims, jnp.float32)
    if pieces:
        entries = entries * levels(stream_key, dims, pieces, -0.22, 0.18)
    return jnp.clip(entries, -bound, bound).astype(held_as)


def setup_inputs(seed: int = 0) -> dict:
    streams_of = jax.random.split(jax.random.key(seed), 6)
    tokens = normal_values(streams_of[0], (SEQS, L, D), 1.0, 6.0, ((0, 4), (1, 8)))
    cotangent = normal_values(streams_of[1], (SEQS, L, D), 1.0, 6.0, ((0, 4), (1, 8)))
    kernel = normal_values(streams_of[2], (L, D), 1.0, 6.0, ((0, 8),))
    first_factor = normal_values(streams_of[3], (GA, GB, GB), GB ** -0.5, 0.375, ((0, 8),))
    second_factor = normal_values(streams_of[4], (GB, GA, GA), GA ** -0.5, 2.0, ((0, 8),))
    return dict(tokens=tokens, cotangent=cotangent, kernel=kernel, first_factor=first_factor, second_factor=second_factor)


def rounded(values):
    return lax.optimization_barrier(values.astype(jnp.bfloat16)).astype(jnp.float32)

def product(spec, left, right):
    return jnp.einsum(spec, left, right)

def reference(tokens, cotangent, kernel, first_factor, second_factor):
    block_width = min(D, 256)
    natural_all = tokens.reshape(SEQS, GA, GB, D)
    upstream_all = cotangent.reshape(SEQS, GA, GB, D)
    kernel_all = kernel.reshape(GB, GA, D)
    first_mat = first_factor.astype(jnp.float32)
    second_mat = second_factor.astype(jnp.float32)

    def over_channels(totals, offset):
        first_grad, second_grad = totals
        kernel_part = lax.dynamic_slice_in_dim(kernel_all, offset, block_width, 2).astype(jnp.float32)
        kernel_grad = jnp.zeros((GB, GA, block_width), jnp.float32)
        for member in range(SEQS):
            natural = lax.dynamic_slice_in_dim(natural_all[member], offset, block_width, 2).astype(jnp.float32)
            upstream = lax.dynamic_slice_in_dim(upstream_all[member], offset, block_width, 2).astype(jnp.float32)
            mixed_in = rounded(product('aqb,abc->aqc', first_mat, natural))
            mixed_up = rounded(product('aqb,abc->aqc', first_mat, upstream))
            forward = product('bpa,abc->bpc', second_mat, mixed_in)
            backward = product('bpa,abc->bpc', second_mat, mixed_up)
            kernel_grad = kernel_grad + forward * backward
            weighted = rounded(kernel_part * forward)
            pulled = rounded(kernel_part * backward)
            second_grad = second_grad + product('bpc,abc->bpa', pulled, mixed_in) + product('bpc,abc->bpa', weighted, mixed_up)
            spread = rounded(product('bpa,bpc->abc', second_mat, weighted))
            pulled_back = rounded(product('bpa,bpc->abc', second_mat, pulled))
            first_grad = first_grad + product('aqc,abc->aqb', pulled_back, natural) + product('aqc,abc->aqb', spread, upstream)
        return ((first_grad, second_grad), kernel_grad)
    initial = (jnp.zeros((GA, GB, GB), jnp.float32), jnp.zeros((GB, GA, GA), jnp.float32))
    offsets = jnp.arange(D // block_width, dtype=jnp.int32) * block_width
    totals, kernel_blocks = lax.scan(over_channels, initial, offsets)
    kernel_total = jnp.moveaxis(kernel_blocks, 0, 2).reshape(L, D)
    seq_share = 1.0 / math.sqrt(SEQS)
    factor_share = 1.0 / math.sqrt(2.0 * D * SEQS)
    grad_kernel = (kernel_total * seq_share).astype(jnp.bfloat16)
    return (grad_kernel, totals[0] * factor_share, totals[1] * factor_share)
```

```python
import functools
import math

import jax
import jax.numpy as jnp
from jax import lax
from jax.experimental import pallas as pl
from jax.experimental.pallas import tpu as pltpu
from jax.sharding import PartitionSpec as P

MESH = pl.DeviceIdType.MESH
BF16 = jnp.bfloat16
F32 = jnp.float32
HALVES = 2
CHUNKS = 4


def dot(left, right):
    return jnp.dot(left, right, preferred_element_type=F32)


def dot_rows(left, right):
    return lax.dot_general(left, right, (((1,), (1,)), ((), ())), preferred_element_type=F32)


def mixer_kernel(
    n,
    groups,
    chunks,
    seq_share,
    factor_share,
    tokens_ref,
    cotangent_ref,
    kernel_ref,
    first_ref,
    second_ref,
    kernel_out,
    first_out,
    second_out,
    first_v,
    tokens_v,
    cotangent_v,
    kernel_v,
    factor_v,
    factor_t_v,
    mixed,
    arrived,
    spread,
    returned,
    own_terms,
    outer_terms,
    pair_terms,
    other_terms,
    final_terms,
    second_acc,
    second_terms,
    first_acc,
    first_terms,
    load_sem,
    first_load_sem,
    store_sem,
    out_send,
    out_recv,
    back_send,
    back_recv,
    outer_send,
    outer_recv,
    pair_send,
    pair_recv,
    final_send,
    final_recv,
    second_send,
    second_recv,
    first_send,
    first_recv,
):
    me = lax.axis_index("seq")
    z = lax.axis_index("dp")
    inner = jnp.logical_and(z >= 1, z <= 2)
    outer = jnp.logical_not(inner)
    rows = first_v.shape[0]
    width = tokens_v.shape[2]
    block = rows // n
    part = block // HALVES

    first_load = pltpu.make_async_copy(first_ref.at[0], first_v, first_load_sem)
    first_load.start()
    loads = []
    for k in range(chunks):
        columns = pl.ds(k * width, width)
        trio = [
            pltpu.make_async_copy(tokens_ref.at[0, :, columns], tokens_v.at[k], load_sem.at[k, 0]),
            pltpu.make_async_copy(cotangent_ref.at[0, :, columns], cotangent_v.at[k], load_sem.at[k, 1]),
            pltpu.make_async_copy(kernel_ref.at[:, columns], kernel_v.at[k], load_sem.at[k, 2]),
        ]
        trio[0].start()
        trio[1].start()
        loads.append(trio)
    for trio in loads:
        trio[2].start()

    barrier = pltpu.get_barrier_semaphore()
    for d in range(1, n):
        pl.semaphore_signal(barrier, inc=1, device_id={"seq": lax.rem(me + d, n)}, device_id_type=MESH)
    for d in range(1, groups):
        pl.semaphore_signal(barrier, inc=1, device_id={"dp": lax.rem(z + d, groups)}, device_id_type=MESH)

    shape = (n, block, rows)
    row_block = lax.broadcasted_iota(jnp.int32, shape, 1) * n
    column = lax.broadcasted_iota(jnp.int32, shape, 2)
    same_block = jnp.logical_and(column >= row_block, column < row_block + n)
    spread_factor = jnp.broadcast_to(second_ref[...][:, None, :], shape)
    transposed = jnp.where(same_block, spread_factor, 0.0).reshape(rows, rows)
    factor_t_v[...] = transposed.astype(BF16)
    factor_v[...] = transposed.T.astype(BF16)
    second_acc[...] = jnp.zeros_like(second_acc)

    def out_copy(k, source, target):
        return pltpu.make_async_remote_copy(
            src_ref=mixed.at[k, target],
            dst_ref=arrived.at[k, source],
            send_sem=out_send.at[k, target],
            recv_sem=out_recv.at[k, source],
            device_id={"seq": target},
            device_id_type=MESH,
        )

    def back_copy(h, k, source, target):
        return pltpu.make_async_remote_copy(
            src_ref=spread.at[h, k, target],
            dst_ref=returned.at[h, k, source],
            send_sem=back_send.at[h, k, target],
            recv_sem=back_recv.at[h, k, source],
            device_id={"seq": target},
            device_id_type=MESH,
        )

    def line_copy(src, dst, send, recv, target):
        return pltpu.make_async_remote_copy(
            src_ref=src,
            dst_ref=dst,
            send_sem=send,
            recv_sem=recv,
            device_id={"dp": target},
            device_id_type=MESH,
        )

    inner_partner = 1 + z // 3
    outer_partner = (z - 1) * 3
    other_inner = 3 - z

    def outer_copy(k):
        return line_copy(pair_terms.at[k], outer_terms.at[k], outer_send.at[k], outer_recv.at[k], inner_partner)

    def pair_copy(k):
        return line_copy(pair_terms.at[k], other_terms.at[k], pair_send.at[k], pair_recv.at[k], other_inner)

    def final_copy(k):
        return line_copy(final_terms.at[k], final_terms.at[k], final_send.at[k], final_recv.at[k], outer_partner)

    def second_copy(source, target):
        return line_copy(
            second_terms.at[source], second_terms.at[source], second_send.at[target], second_recv.at[source], target
        )

    def first_copy(h, source, target):
        return line_copy(
            first_terms.at[h, source], first_terms.at[h, source], first_send.at[h, target], first_recv.at[h, source], target
        )

    def peers(action):
        def step(d, carry):
            action(lax.rem(me + d, n))
            return carry

        lax.fori_loop(1, n, step, 0)

    def line_peers(action):
        for d in range(1, groups):
            action(lax.rem(z + d, groups))

    first_load.wait()
    for k in range(chunks):
        loads[k][0].wait()
        loads[k][1].wait()
        mixed[k, :, 0] = dot(first_v[...], tokens_v[k]).astype(BF16).reshape(n, block, width)
        mixed[k, :, 1] = dot(first_v[...], cotangent_v[k]).astype(BF16).reshape(n, block, width)
        if k == 0:
            pl.semaphore_wait(barrier, n + groups - 2)
        peers(lambda target, k=k: out_copy(k, me, target).start())
        arrived[k, me] = mixed[k, me]
    for trio in loads:
        trio[2].wait()

    def make_pair(k):
        outer_copy(k).wait_recv()
        pair_terms[k] = (own_terms[k] + outer_terms[k].astype(F32)).astype(BF16)
        pair_copy(k).start()

    def make_final(k):
        pair_copy(k).wait_recv()
        total = pair_terms[k].astype(F32) + other_terms[k].astype(F32)
        final_terms[k] = (total * seq_share).astype(BF16)
        final_copy(k).start()

    def transform(k, carry):
        peers(lambda source: out_copy(k, source, me).wait_recv())
        mixed_in = arrived[k, :, 0].reshape(rows, width)
        mixed_up = arrived[k, :, 1].reshape(rows, width)
        forward = dot(factor_v[...], mixed_in)
        backward = dot(factor_v[...], mixed_up)
        terms = forward * backward
        gains = kernel_v[k].astype(F32)
        weighted = (gains * forward).astype(BF16)
        pulled = (gains * backward).astype(BF16)
        back = dot(factor_t_v[...], pulled).astype(BF16).reshape(n, HALVES, part, width)
        ahead = dot(factor_t_v[...], weighted).astype(BF16).reshape(n, HALVES, part, width)
        for h in range(HALVES):
            spread[h, k, :, 0] = back[:, h]
            spread[h, k, :, 1] = ahead[:, h]
        peers(lambda target: back_copy(0, k, me, target).start())

        @pl.when(outer)
        def _():
            pair_terms[k] = terms.astype(BF16)
            outer_copy(k).start()

        @pl.when(inner)
        def _():
            own_terms[k] = terms

        for h in range(HALVES):
            returned[h, k, me] = spread[h, k, me]
        second_acc[...] += dot_rows(mixed_in, pulled) + dot_rows(mixed_up, weighted)

        @pl.when(jnp.logical_and(inner, k >= 1))
        def _():
            make_pair(k - 1)

        @pl.when(jnp.logical_and(inner, k >= 2))
        def _():
            make_final(k - 2)

        return carry

    lax.fori_loop(0, chunks, transform, 0)
    for h in range(1, HALVES):
        for k in range(chunks):
            peers(lambda target, h=h, k=k: back_copy(h, k, me, target).start())

    second_terms[z] = jnp.sum(
        jnp.where(same_block, second_acc[...].reshape(shape), 0.0), axis=1
    )
    line_peers(lambda target: second_copy(z, target).start())

    @pl.when(inner)
    def _():
        make_pair(chunks - 1)
        if chunks >= 2:
            make_final(chunks - 2)

    for h in range(HALVES):
        first_acc[...] = jnp.zeros_like(first_acc)

        def gather(k, carry, h=h):
            peers(lambda source: back_copy(h, k, source, me).wait_recv())
            back = returned[h, k, :, 0].reshape(n * part, width)
            ahead = returned[h, k, :, 1].reshape(n * part, width)
            first_acc[...] += dot_rows(back, tokens_v[k]) + dot_rows(ahead, cotangent_v[k])
            return carry

        lax.fori_loop(0, chunks, gather, 0)
        first_terms[h, z] = first_acc[...].astype(BF16)
        line_peers(lambda target, h=h: first_copy(h, z, target).start())
        if h == 0:

            @pl.when(inner)
            def _():
                make_final(chunks - 1)

    stores = []
    for k in range(chunks):

        @pl.when(outer)
        def _():
            final_copy(k).wait_recv()

        stores.append(
            pltpu.make_async_copy(final_terms.at[k], kernel_out.at[:, pl.ds(k * width, width)], store_sem.at[k])
        )
        stores[-1].start()

    line_peers(lambda source: second_copy(source, z).wait_recv())
    second_out[...] = jnp.sum(second_terms[...], axis=0) * factor_share
    for h in range(HALVES):
        line_peers(lambda source, h=h: first_copy(h, source, z).wait_recv())
        total = jnp.sum(first_terms[h].astype(F32), axis=0) * factor_share
        first_out[:, h] = total.reshape(n, part, rows)

    for store in stores:
        store.wait()
    for k in range(chunks):
        peers(lambda target, k=k: out_copy(k, me, target).wait_send())
        for h in range(HALVES):
            peers(lambda target, h=h, k=k: back_copy(h, k, me, target).wait_send())

        @pl.when(outer)
        def _():
            outer_copy(k).wait_send()

        @pl.when(inner)
        def _():
            pair_copy(k).wait_send()
            final_copy(k).wait_send()

    line_peers(lambda target: second_copy(z, target).wait_send())
    for h in range(HALVES):
        line_peers(lambda target, h=h: first_copy(h, z, target).wait_send())


def fused(n, groups, tokens, cotangent, kernel, first_factor, second_factor):
    rows, channels = tokens.shape[1:]
    chunks = CHUNKS
    width = channels // chunks
    block = rows // n
    part = block // HALVES
    seq_share = 1.0 / math.sqrt(groups)
    factor_share = 1.0 / math.sqrt(2.0 * channels * groups)
    second = jnp.transpose(second_factor, (2, 0, 1)).reshape(n, rows).astype(F32)
    any_spec = pl.BlockSpec(memory_space=pl.ANY)
    vmem_spec = pl.BlockSpec(memory_space=pltpu.VMEM)
    dma = pltpu.SemaphoreType.DMA
    kernel_grad, first_grad, second_grad = pl.pallas_call(
        functools.partial(mixer_kernel, n, groups, chunks, seq_share, factor_share),
        out_shape=(
            jax.ShapeDtypeStruct((rows, channels), BF16),
            jax.ShapeDtypeStruct((n, HALVES, part, rows), F32),
            jax.ShapeDtypeStruct((n, rows), F32),
        ),
        in_specs=[any_spec] * 4 + [vmem_spec],
        out_specs=(any_spec, vmem_spec, vmem_spec),
        scratch_shapes=[
            pltpu.VMEM((rows, rows), BF16),
            pltpu.VMEM((chunks, rows, width), BF16),
            pltpu.VMEM((chunks, rows, width), BF16),
            pltpu.VMEM((chunks, rows, width), BF16),
            pltpu.VMEM((rows, rows), BF16),
            pltpu.VMEM((rows, rows), BF16),
            pltpu.VMEM((chunks, n, 2, block, width), BF16),
            pltpu.VMEM((chunks, n, 2, block, width), BF16),
            pltpu.VMEM((HALVES, chunks, n, 2, part, width), BF16),
            pltpu.VMEM((HALVES, chunks, n, 2, part, width), BF16),
            pltpu.VMEM((chunks, rows, width), F32),
            pltpu.VMEM((chunks, rows, width), BF16),
            pltpu.VMEM((chunks, rows, width), BF16),
            pltpu.VMEM((chunks, rows, width), BF16),
            pltpu.VMEM((chunks, rows, width), BF16),
            pltpu.VMEM((rows, rows), F32),
            pltpu.VMEM((groups, n, rows), F32),
            pltpu.VMEM((n * part, rows), F32),
            pltpu.VMEM((HALVES, groups, n * part, rows), BF16),
            dma((chunks, 3)),
            dma,
            dma((chunks,)),
            dma((chunks, n)),
            dma((chunks, n)),
            dma((HALVES, chunks, n)),
            dma((HALVES, chunks, n)),
            dma((chunks,)),
            dma((chunks,)),
            dma((chunks,)),
            dma((chunks,)),
            dma((chunks,)),
            dma((chunks,)),
            dma((groups,)),
            dma((groups,)),
            dma((HALVES, groups)),
            dma((HALVES, groups)),
        ],
        compiler_params=pltpu.CompilerParams(
            collective_id=0, has_side_effects=True, vmem_limit_bytes=48 * 1024 * 1024
        ),
        cost_estimate=pl.CostEstimate(
            flops=16 * rows * rows * channels, bytes_accessed=8 * rows * channels, transcendentals=0
        ),
    )(tokens, cotangent, kernel, first_factor, second)
    second_grad = second_grad.reshape(n, block, n).transpose(1, 2, 0)
    return kernel_grad, first_grad.reshape(1, rows, rows), second_grad


def separate(tokens, cotangent, kernel, first_factor, second_factor):
    local_rows = tokens.shape[1]
    channels = tokens.shape[2]
    column_blocks = second_factor.shape[0]
    mixed_in = jnp.einsum(
        "aqb,abc->aqc", first_factor, tokens, preferred_element_type=jnp.float32
    ).astype(jnp.bfloat16)
    mixed_up = jnp.einsum(
        "aqb,abc->aqc", first_factor, cotangent, preferred_element_type=jnp.float32
    ).astype(jnp.bfloat16)
    arrived_in = lax.all_to_all(mixed_in, "seq", split_axis=1, concat_axis=0, tiled=True)
    arrived_up = lax.all_to_all(mixed_up, "seq", split_axis=1, concat_axis=0, tiled=True)
    forward = jnp.einsum(
        "bpa,abc->bpc", second_factor, arrived_in, preferred_element_type=jnp.float32
    )
    backward = jnp.einsum(
        "bpa,abc->bpc", second_factor, arrived_up, preferred_element_type=jnp.float32
    )
    arrived_in, arrived_up, forward, backward = (arrived_in, arrived_up, forward, backward)
    kernel_local = kernel.reshape(column_blocks, -1, channels)
    kernel_grad = forward * backward
    weighted = (kernel_local * forward).astype(jnp.bfloat16)
    pulled = (kernel_local * backward).astype(jnp.bfloat16)
    second_grad = jnp.einsum(
        "bpc,abc->bpa", pulled, arrived_in, preferred_element_type=jnp.float32
    ) + jnp.einsum("bpc,abc->bpa", weighted, arrived_up, preferred_element_type=jnp.float32)
    spread = jnp.einsum(
        "bpa,bpc->abc", second_factor, weighted, preferred_element_type=jnp.float32
    ).astype(jnp.bfloat16)
    pulled_back = jnp.einsum(
        "bpa,bpc->abc", second_factor, pulled, preferred_element_type=jnp.float32
    ).astype(jnp.bfloat16)
    seq_share = 1.0 / math.sqrt(lax.axis_size("dp"))
    factor_share = 1.0 / math.sqrt(2.0 * channels * lax.axis_size("dp"))
    returned, returned_back = (
        lax.all_to_all(spread, "seq", split_axis=0, concat_axis=1, tiled=True),
        lax.all_to_all(pulled_back, "seq", split_axis=0, concat_axis=1, tiled=True),
    )
    first_grad = jnp.einsum(
        "aqc,abc->aqb", returned_back, tokens, preferred_element_type=jnp.float32
    ) + jnp.einsum("aqc,abc->aqb", returned, cotangent, preferred_element_type=jnp.float32)
    kernel_total, first_total, second_total = lax.psum((kernel_grad, first_grad, second_grad), "dp")
    kernel_out = (kernel_total * seq_share).astype(jnp.bfloat16)
    return (
        kernel_out.reshape(local_rows, channels),
        first_total * factor_share,
        second_total * factor_share,
    )


def shards(tokens, cotangent, kernel, first_factor, second_factor):
    n = lax.axis_size("seq")
    groups = lax.axis_size("dp")
    rows, channels = tokens.shape[1:]
    fits = (
        groups == 4
        and first_factor.shape[0] == 1
        and second_factor.shape[1] == n
        and second_factor.shape[0] % (16 * HALVES) == 0
        and channels % (128 * CHUNKS) == 0
        and rows == n * second_factor.shape[0]
    )
    arguments = (tokens, cotangent, kernel, first_factor, second_factor)
    return fused(n, groups, *arguments) if fits else separate(*arguments)


def solution(mesh):
    in_specs = (
        P("dp", "seq", None),
        P("dp", "seq", None),
        P("seq", None),
        P("seq", None, None),
        P("seq", None, None),
    )
    out_specs = (P("seq", None), P("seq", None, None), P("seq", None, None))
    return jax.shard_map(shards, mesh=mesh, in_specs=in_specs, out_specs=out_specs, check_vma=False)
```

```python
import functools
import math

import jax
import jax.numpy as jnp
from jax import lax
from jax.experimental import pallas as pl
from jax.experimental.pallas import tpu as pltpu
from jax.sharding import PartitionSpec as P

MESH = pl.DeviceIdType.MESH
BF16 = jnp.bfloat16
F32 = jnp.float32
HALVES = 2
CHUNKS = 4
AHEAD = 2


def dot(left, right):
    return jnp.dot(left, right, preferred_element_type=F32)


def dot_rows(left, right):
    return lax.dot_general(left, right, (((1,), (1,)), ((), ())), preferred_element_type=F32)


def mixer_kernel(
    n,
    groups,
    chunks,
    seq_share,
    factor_share,
    tokens_ref,
    cotangent_ref,
    kernel_ref,
    first_ref,
    second_ref,
    kernel_out,
    first_out,
    second_out,
    first_v,
    tokens_v,
    cotangent_v,
    kernel_v,
    factor_v,
    factor_t_v,
    mixed,
    arrived,
    spread,
    returned,
    own_terms,
    outer_terms,
    pair_terms,
    other_terms,
    final_terms,
    second_acc,
    second_terms,
    first_acc,
    first_terms,
    load_sem,
    first_load_sem,
    store_sem,
    out_send,
    out_recv,
    back_send,
    back_recv,
    outer_send,
    outer_recv,
    pair_send,
    pair_recv,
    final_send,
    final_recv,
    second_send,
    second_recv,
    first_send,
    first_recv,
):
    me = lax.axis_index("seq")
    z = lax.axis_index("dp")
    inner = jnp.logical_and(z >= 1, z <= 2)
    outer = jnp.logical_not(inner)
    rows = first_v.shape[0]
    width = tokens_v.shape[2]
    block = rows // n
    part = block // HALVES

    first_load = pltpu.make_async_copy(first_ref.at[0], first_v, first_load_sem)
    first_load.start()
    loads = []
    for k in range(chunks):
        columns = pl.ds(k * width, width)
        trio = [
            pltpu.make_async_copy(tokens_ref.at[0, :, columns], tokens_v.at[k], load_sem.at[k, 0]),
            pltpu.make_async_copy(cotangent_ref.at[0, :, columns], cotangent_v.at[k], load_sem.at[k, 1]),
            pltpu.make_async_copy(kernel_ref.at[:, columns], kernel_v.at[k], load_sem.at[k, 2]),
        ]
        trio[0].start()
        trio[1].start()
        loads.append(trio)
    for trio in loads:
        trio[2].start()

    barrier = pltpu.get_barrier_semaphore()
    for d in range(1, n):
        pl.semaphore_signal(barrier, inc=1, device_id={"seq": lax.rem(me + d, n)}, device_id_type=MESH)
    for d in range(1, groups):
        pl.semaphore_signal(barrier, inc=1, device_id={"dp": lax.rem(z + d, groups)}, device_id_type=MESH)

    shape = (n, block, rows)
    row_block = lax.broadcasted_iota(jnp.int32, shape, 1) * n
    column = lax.broadcasted_iota(jnp.int32, shape, 2)
    same_block = jnp.logical_and(column >= row_block, column < row_block + n)
    spread_factor = jnp.broadcast_to(second_ref[...][:, None, :], shape)
    transposed = jnp.where(same_block, spread_factor, 0.0).reshape(rows, rows)
    factor_t_v[...] = transposed.astype(BF16)
    factor_v[...] = transposed.T.astype(BF16)
    second_acc[...] = jnp.zeros_like(second_acc)

    def out_copy(k, source, target):
        return pltpu.make_async_remote_copy(
            src_ref=mixed.at[k, target],
            dst_ref=arrived.at[k, source],
            send_sem=out_send.at[k, target],
            recv_sem=out_recv.at[k, source],
            device_id={"seq": target},
            device_id_type=MESH,
        )

    def back_copy(h, k, source, target):
        return pltpu.make_async_remote_copy(
            src_ref=spread.at[h, k, target],
            dst_ref=returned.at[h, k, source],
            send_sem=back_send.at[h, k, target],
            recv_sem=back_recv.at[h, k, source],
            device_id={"seq": target},
            device_id_type=MESH,
        )

    def line_copy(src, dst, send, recv, target):
        return pltpu.make_async_remote_copy(
            src_ref=src,
            dst_ref=dst,
            send_sem=send,
            recv_sem=recv,
            device_id={"dp": target},
            device_id_type=MESH,
        )

    inner_partner = 1 + z // 3
    outer_partner = (z - 1) * 3
    other_inner = 3 - z

    def outer_copy(k):
        return line_copy(pair_terms.at[k], outer_terms.at[k], outer_send.at[k], outer_recv.at[k], inner_partner)

    def pair_copy(k):
        return line_copy(pair_terms.at[k], other_terms.at[k], pair_send.at[k], pair_recv.at[k], other_inner)

    def final_copy(k):
        return line_copy(final_terms.at[k], final_terms.at[k], final_send.at[k], final_recv.at[k], outer_partner)

    def second_copy(source, target):
        return line_copy(
            second_terms.at[source], second_terms.at[source], second_send.at[target], second_recv.at[source], target
        )

    def first_copy(h, source, target):
        return line_copy(
            first_terms.at[h, source], first_terms.at[h, source], first_send.at[h, target], first_recv.at[h, source], target
        )

    def peers(action):
        def step(d, carry):
            action(lax.rem(me + d, n))
            return carry

        lax.fori_loop(1, n, step, 0)

    def line_peers(action):
        for d in range(1, groups):
            action(lax.rem(z + d, groups))

    first_load.wait()
    for k in range(chunks):
        loads[k][0].wait()
        loads[k][1].wait()
        mixed[k, :, 0] = dot(first_v[...], tokens_v[k]).astype(BF16).reshape(n, block, width)
        mixed[k, :, 1] = dot(first_v[...], cotangent_v[k]).astype(BF16).reshape(n, block, width)
        if k == 0:
            pl.semaphore_wait(barrier, n + groups - 2)
        if k < AHEAD:
            peers(lambda target, k=k: out_copy(k, me, target).start())
        arrived[k, me] = mixed[k, me]
    for trio in loads:
        trio[2].wait()

    def make_pair(k):
        outer_copy(k).wait_recv()
        pair_terms[k] = (own_terms[k] + outer_terms[k].astype(F32)).astype(BF16)
        pair_copy(k).start()

    def make_final(k):
        pair_copy(k).wait_recv()
        total = pair_terms[k].astype(F32) + other_terms[k].astype(F32)
        final_terms[k] = (total * seq_share).astype(BF16)
        final_copy(k).start()

    def transform(k, carry):
        peers(lambda source: out_copy(k, source, me).wait_recv())

        @pl.when(k + AHEAD < chunks)
        def _():
            peers(lambda target: out_copy(k + AHEAD, me, target).start())

        mixed_in = arrived[k, :, 0].reshape(rows, width)
        mixed_up = arrived[k, :, 1].reshape(rows, width)
        forward = dot(factor_v[...], mixed_in)
        backward = dot(factor_v[...], mixed_up)
        terms = forward * backward
        gains = kernel_v[k].astype(F32)
        weighted = (gains * forward).astype(BF16)
        pulled = (gains * backward).astype(BF16)
        back = dot(factor_t_v[...], pulled).astype(BF16).reshape(n, HALVES, part, width)
        ahead = dot(factor_t_v[...], weighted).astype(BF16).reshape(n, HALVES, part, width)
        for h in range(HALVES):
            spread[h, k, :, 0] = back[:, h]
            spread[h, k, :, 1] = ahead[:, h]
        peers(lambda target: back_copy(0, k, me, target).start())

        @pl.when(outer)
        def _():
            pair_terms[k] = terms.astype(BF16)
            outer_copy(k).start()

        @pl.when(inner)
        def _():
            own_terms[k] = terms

        for h in range(HALVES):
            returned[h, k, me] = spread[h, k, me]
        second_acc[...] += dot_rows(mixed_in, pulled) + dot_rows(mixed_up, weighted)

        @pl.when(jnp.logical_and(inner, k >= 1))
        def _():
            make_pair(k - 1)

        @pl.when(jnp.logical_and(inner, k >= 2))
        def _():
            make_final(k - 2)

        return carry

    lax.fori_loop(0, chunks, transform, 0)
    for h in range(1, HALVES):
        for k in range(chunks):
            peers(lambda target, h=h, k=k: back_copy(h, k, me, target).start())

    second_terms[z] = jnp.sum(
        jnp.where(same_block, second_acc[...].reshape(shape), 0.0), axis=1
    )
    line_peers(lambda target: second_copy(z, target).start())

    @pl.when(inner)
    def _():
        make_pair(chunks - 1)
        if chunks >= 2:
            make_final(chunks - 2)

    for h in range(HALVES):
        first_acc[...] = jnp.zeros_like(first_acc)

        def gather(k, carry, h=h):
            peers(lambda source: back_copy(h, k, source, me).wait_recv())
            back = returned[h, k, :, 0].reshape(n * part, width)
            ahead = returned[h, k, :, 1].reshape(n * part, width)
            first_acc[...] += dot_rows(back, tokens_v[k]) + dot_rows(ahead, cotangent_v[k])
            return carry

        lax.fori_loop(0, chunks, gather, 0)
        first_terms[h, z] = first_acc[...].astype(BF16)
        line_peers(lambda target, h=h: first_copy(h, z, target).start())
        if h == 0:

            @pl.when(inner)
            def _():
                make_final(chunks - 1)

    stores = []
    for k in range(chunks):

        @pl.when(outer)
        def _():
            final_copy(k).wait_recv()

        stores.append(
            pltpu.make_async_copy(final_terms.at[k], kernel_out.at[:, pl.ds(k * width, width)], store_sem.at[k])
        )
        stores[-1].start()

    line_peers(lambda source: second_copy(source, z).wait_recv())
    second_out[...] = jnp.sum(second_terms[...], axis=0) * factor_share
    for h in range(HALVES):
        line_peers(lambda source, h=h: first_copy(h, source, z).wait_recv())
        total = jnp.sum(first_terms[h].astype(F32), axis=0) * factor_share
        first_out[:, h] = total.reshape(n, part, rows)

    for store in stores:
        store.wait()
    for k in range(chunks):
        peers(lambda target, k=k: out_copy(k, me, target).wait_send())
        for h in range(HALVES):
            peers(lambda target, h=h, k=k: back_copy(h, k, me, target).wait_send())

        @pl.when(outer)
        def _():
            outer_copy(k).wait_send()

        @pl.when(inner)
        def _():
            pair_copy(k).wait_send()
            final_copy(k).wait_send()

    line_peers(lambda target: second_copy(z, target).wait_send())
    for h in range(HALVES):
        line_peers(lambda target, h=h: first_copy(h, z, target).wait_send())


def fused(n, groups, tokens, cotangent, kernel, first_factor, second_factor):
    rows, channels = tokens.shape[1:]
    chunks = CHUNKS
    width = channels // chunks
    block = rows // n
    part = block // HALVES
    seq_share = 1.0 / math.sqrt(groups)
    factor_share = 1.0 / math.sqrt(2.0 * channels * groups)
    second = jnp.transpose(second_factor, (2, 0, 1)).reshape(n, rows).astype(F32)
    any_spec = pl.BlockSpec(memory_space=pltpu.HBM)
    vmem_spec = pl.BlockSpec(memory_space=pltpu.VMEM)
    dma = pltpu.SemaphoreType.DMA
    kernel_grad, first_grad, second_grad = pl.pallas_call(
        functools.partial(mixer_kernel, n, groups, chunks, seq_share, factor_share),
        out_shape=(
            jax.ShapeDtypeStruct((rows, channels), BF16),
            jax.ShapeDtypeStruct((n, HALVES, part, rows), F32),
            jax.ShapeDtypeStruct((n, rows), F32),
        ),
        in_specs=[any_spec] * 4 + [vmem_spec],
        out_specs=(any_spec, vmem_spec, vmem_spec),
        scratch_shapes=[
            pltpu.VMEM((rows, rows), BF16),
            pltpu.VMEM((chunks, rows, width), BF16),
            pltpu.VMEM((chunks, rows, width), BF16),
            pltpu.VMEM((chunks, rows, width), BF16),
            pltpu.VMEM((rows, rows), BF16),
            pltpu.VMEM((rows, rows), BF16),
            pltpu.VMEM((chunks, n, 2, block, width), BF16),
            pltpu.VMEM((chunks, n, 2, block, width), BF16),
            pltpu.VMEM((HALVES, chunks, n, 2, part, width), BF16),
            pltpu.VMEM((HALVES, chunks, n, 2, part, width), BF16),
            pltpu.VMEM((chunks, rows, width), F32),
            pltpu.VMEM((chunks, rows, width), BF16),
            pltpu.VMEM((chunks, rows, width), BF16),
            pltpu.VMEM((chunks, rows, width), BF16),
            pltpu.VMEM((chunks, rows, width), BF16),
            pltpu.VMEM((rows, rows), F32),
            pltpu.VMEM((groups, n, rows), F32),
            pltpu.VMEM((n * part, rows), F32),
            pltpu.VMEM((HALVES, groups, n * part, rows), BF16),
            dma((chunks, 3)),
            dma,
            dma((chunks,)),
            dma((chunks, n)),
            dma((chunks, n)),
            dma((HALVES, chunks, n)),
            dma((HALVES, chunks, n)),
            dma((chunks,)),
            dma((chunks,)),
            dma((chunks,)),
            dma((chunks,)),
            dma((chunks,)),
            dma((chunks,)),
            dma((groups,)),
            dma((groups,)),
            dma((HALVES, groups)),
            dma((HALVES, groups)),
        ],
        compiler_params=pltpu.CompilerParams(
            collective_id=0, has_side_effects=True, vmem_limit_bytes=48 * 1024 * 1024
        ),
        cost_estimate=pl.CostEstimate(
            flops=16 * rows * rows * channels, bytes_accessed=8 * rows * channels, transcendentals=0
        ),
    )(tokens, cotangent, kernel, first_factor, second)
    second_grad = second_grad.reshape(n, block, n).transpose(1, 2, 0)
    return kernel_grad, first_grad.reshape(1, rows, rows), second_grad


def separate(tokens, cotangent, kernel, first_factor, second_factor):
    local_rows = tokens.shape[1]
    channels = tokens.shape[2]
    column_blocks = second_factor.shape[0]
    mixed_in = jnp.einsum(
        "aqb,abc->aqc", first_factor, tokens, preferred_element_type=jnp.float32
    ).astype(jnp.bfloat16)
    mixed_up = jnp.einsum(
        "aqb,abc->aqc", first_factor, cotangent, preferred_element_type=jnp.float32
    ).astype(jnp.bfloat16)
    arrived_in = lax.all_to_all(mixed_in, "seq", split_axis=1, concat_axis=0, tiled=True)
    arrived_up = lax.all_to_all(mixed_up, "seq", split_axis=1, concat_axis=0, tiled=True)
    forward = jnp.einsum(
        "bpa,abc->bpc", second_factor, arrived_in, preferred_element_type=jnp.float32
    )
    backward = jnp.einsum(
        "bpa,abc->bpc", second_factor, arrived_up, preferred_element_type=jnp.float32
    )
    arrived_in, arrived_up, forward, backward = (arrived_in, arrived_up, forward, backward)
    kernel_local = kernel.reshape(column_blocks, -1, channels)
    kernel_grad = forward * backward
    weighted = (kernel_local * forward).astype(jnp.bfloat16)
    pulled = (kernel_local * backward).astype(jnp.bfloat16)
    second_grad = jnp.einsum(
        "bpc,abc->bpa", pulled, arrived_in, preferred_element_type=jnp.float32
    ) + jnp.einsum("bpc,abc->bpa", weighted, arrived_up, preferred_element_type=jnp.float32)
    spread = jnp.einsum(
        "bpa,bpc->abc", second_factor, weighted, preferred_element_type=jnp.float32
    ).astype(jnp.bfloat16)
    pulled_back = jnp.einsum(
        "bpa,bpc->abc", second_factor, pulled, preferred_element_type=jnp.float32
    ).astype(jnp.bfloat16)
    seq_share = 1.0 / math.sqrt(lax.axis_size("dp"))
    factor_share = 1.0 / math.sqrt(2.0 * channels * lax.axis_size("dp"))
    returned, returned_back = (
        lax.all_to_all(spread, "seq", split_axis=0, concat_axis=1, tiled=True),
        lax.all_to_all(pulled_back, "seq", split_axis=0, concat_axis=1, tiled=True),
    )
    first_grad = jnp.einsum(
        "aqc,abc->aqb", returned_back, tokens, preferred_element_type=jnp.float32
    ) + jnp.einsum("aqc,abc->aqb", returned, cotangent, preferred_element_type=jnp.float32)
    kernel_total, first_total, second_total = lax.psum((kernel_grad, first_grad, second_grad), "dp")
    kernel_out = (kernel_total * seq_share).astype(jnp.bfloat16)
    return (
        kernel_out.reshape(local_rows, channels),
        first_total * factor_share,
        second_total * factor_share,
    )


def shards(tokens, cotangent, kernel, first_factor, second_factor):
    n = lax.axis_size("seq")
    groups = lax.axis_size("dp")
    rows, channels = tokens.shape[1:]
    fits = (
        groups == 4
        and first_factor.shape[0] == 1
        and second_factor.shape[1] == n
        and second_factor.shape[0] % (16 * HALVES) == 0
        and channels % (128 * CHUNKS) == 0
        and rows == n * second_factor.shape[0]
    )
    arguments = (tokens, cotangent, kernel, first_factor, second_factor)
    return fused(n, groups, *arguments) if fits else separate(*arguments)


def solution(mesh):
    in_specs = (
        P("dp", "seq", None),
        P("dp", "seq", None),
        P("seq", None),
        P("seq", None, None),
        P("seq", None, None),
    )
    out_specs = (P("seq", None), P("seq", None, None), P("seq", None, None))
    return jax.shard_map(shards, mesh=mesh, in_specs=in_specs, out_specs=out_specs, check_vma=False)
```

```python
import functools
import math

import jax
import jax.numpy as jnp
from jax import lax
from jax.experimental import pallas as pl
from jax.experimental.pallas import tpu as pltpu
from jax.sharding import PartitionSpec as P

MESH = pl.DeviceIdType.MESH
BF16 = jnp.bfloat16
F32 = jnp.float32
PARTS = 4
CHUNKS = 4


def dot(left, right):
    return jnp.dot(left, right, preferred_element_type=F32)


def dot_rows(left, right):
    return lax.dot_general(left, right, (((1,), (1,)), ((), ())), preferred_element_type=F32)


def flipped(index, mask):
    result = 0
    for bit in (1, 2, 4):
        own, flip = lax.rem(index // bit, 2), lax.rem(mask // bit, 2)
        result = result + bit * (own + flip - 2 * own * flip)
    return result


def mixer_kernel(
    n,
    groups,
    chunks,
    seq_share,
    factor_share,
    tokens_ref,
    cotangent_ref,
    kernel_ref,
    first_ref,
    second_ref,
    kernel_out,
    first_out,
    second_out,
    first_v,
    tokens_v,
    cotangent_v,
    kernel_v,
    factor_v,
    factor_t_v,
    mixed,
    arrived,
    spread,
    returned,
    own_terms,
    outer_terms,
    pair_terms,
    other_terms,
    final_terms,
    second_acc,
    second_terms,
    first_acc,
    first_terms,
    load_sem,
    first_load_sem,
    store_sem,
    out_send,
    out_recv,
    back_send,
    back_recv,
    late_send,
    late_recv,
    outer_send,
    outer_recv,
    pair_send,
    pair_recv,
    final_send,
    final_recv,
    second_send,
    second_recv,
    first_send,
    first_recv,
):
    me = lax.axis_index("seq")
    z = lax.axis_index("dp")
    inner = jnp.logical_and(z >= 1, z <= 2)
    outer = jnp.logical_not(inner)
    rows = first_v.shape[0]
    width = tokens_v.shape[2]
    block = rows // n
    part = block // PARTS

    first_load = pltpu.make_async_copy(first_ref.at[0], first_v, first_load_sem)
    first_load.start()
    loads = []
    for k in range(chunks):
        columns = pl.ds(k * width, width)
        trio = [
            pltpu.make_async_copy(tokens_ref.at[0, :, columns], tokens_v.at[k], load_sem.at[k, 0]),
            pltpu.make_async_copy(cotangent_ref.at[0, :, columns], cotangent_v.at[k], load_sem.at[k, 1]),
            pltpu.make_async_copy(kernel_ref.at[:, columns], kernel_v.at[k], load_sem.at[k, 2]),
        ]
        trio[0].start()
        trio[1].start()
        loads.append(trio)
    for trio in loads:
        trio[2].start()

    barrier = pltpu.get_barrier_semaphore()
    for d in range(1, n):
        pl.semaphore_signal(barrier, inc=1, device_id={"seq": lax.rem(me + d, n)}, device_id_type=MESH)
    for d in range(1, groups):
        pl.semaphore_signal(barrier, inc=1, device_id={"dp": lax.rem(z + d, groups)}, device_id_type=MESH)

    shape = (n, block, rows)
    row_block = lax.broadcasted_iota(jnp.int32, shape, 1) * n
    column = lax.broadcasted_iota(jnp.int32, shape, 2)
    same_block = jnp.logical_and(column >= row_block, column < row_block + n)
    pick_block = lax.broadcasted_iota(jnp.int32, (block, rows), 0) * n
    pick_column = lax.broadcasted_iota(jnp.int32, (block, rows), 1)
    picks = [(pick_column == pick_block + p).astype(F32).astype(BF16) for p in range(n)]
    second = sum(dot(second_ref[p], picks[p]) for p in range(n))
    spread_factor = jnp.broadcast_to(second[:, None, :], shape)
    transposed = jnp.where(same_block, spread_factor, 0.0).reshape(rows, rows)
    factor_t_v[...] = transposed.astype(BF16)
    factor_v[...] = transposed.T.astype(BF16)
    second_acc[...] = jnp.zeros_like(second_acc)

    def out_copy(k, source, target):
        return pltpu.make_async_remote_copy(
            src_ref=mixed.at[k, target],
            dst_ref=arrived.at[k, source],
            send_sem=out_send.at[k, target],
            recv_sem=out_recv.at[k, source],
            device_id={"seq": target},
            device_id_type=MESH,
        )

    def back_copy(k, source, target):
        return pltpu.make_async_remote_copy(
            src_ref=spread.at[0, target, k],
            dst_ref=returned.at[0, source, k],
            send_sem=back_send.at[k, target],
            recv_sem=back_recv.at[k, source],
            device_id={"seq": target},
            device_id_type=MESH,
        )

    def late_copy(h, source, target):
        return pltpu.make_async_remote_copy(
            src_ref=spread.at[h, target],
            dst_ref=returned.at[h, source],
            send_sem=late_send.at[h, target],
            recv_sem=late_recv.at[h, source],
            device_id={"seq": target},
            device_id_type=MESH,
        )

    def line_copy(src, dst, send, recv, target):
        return pltpu.make_async_remote_copy(
            src_ref=src,
            dst_ref=dst,
            send_sem=send,
            recv_sem=recv,
            device_id={"dp": target},
            device_id_type=MESH,
        )

    inner_partner = 1 + z // 3
    outer_partner = (z - 1) * 3
    other_inner = 3 - z

    def outer_copy(k):
        return line_copy(pair_terms.at[k], outer_terms.at[k], outer_send.at[k], outer_recv.at[k], inner_partner)

    def pair_copy(k):
        return line_copy(pair_terms.at[k], other_terms.at[k], pair_send.at[k], pair_recv.at[k], other_inner)

    def final_copy(k):
        return line_copy(final_terms.at[k], final_terms.at[k], final_send.at[k], final_recv.at[k], outer_partner)

    def second_copy(source, target):
        return line_copy(
            second_terms.at[source], second_terms.at[source], second_send.at[target], second_recv.at[source], target
        )

    def first_copy(h, source, target):
        return line_copy(
            first_terms.at[h, source], first_terms.at[h, source], first_send.at[h, target], first_recv.at[h, source], target
        )

    def peers(action):
        def step(i, carry):
            action(flipped(me, 1 + lax.rem(2 * i + 1, n - 1)))
            return carry

        lax.fori_loop(0, n - 1, step, 0)

    def line_peers(action):
        for d in range(1, groups):
            action(lax.rem(z + d, groups))

    first_load.wait()
    for k in range(chunks):
        loads[k][0].wait()
        loads[k][1].wait()
        mixed[k, :, 0] = dot(first_v[...], tokens_v[k]).astype(BF16).reshape(n, block, width)
        mixed[k, :, 1] = dot(first_v[...], cotangent_v[k]).astype(BF16).reshape(n, block, width)
        if k == 0:
            pl.semaphore_wait(barrier, n + groups - 2)
        peers(lambda target, k=k: out_copy(k, me, target).start())
        arrived[k, me] = mixed[k, me]
    for trio in loads:
        trio[2].wait()

    def make_pair(k):
        outer_copy(k).wait_recv()
        pair_terms[k] = (own_terms[k] + outer_terms[k].astype(F32)).astype(BF16)
        pair_copy(k).start()

    def make_final(k):
        pair_copy(k).wait_recv()
        total = pair_terms[k].astype(F32) + other_terms[k].astype(F32)
        final_terms[k] = (total * seq_share).astype(BF16)
        final_copy(k).start()

    def transform(k, carry):
        peers(lambda source: out_copy(k, source, me).wait_recv())
        mixed_in = arrived[k, :, 0].reshape(rows, width)
        mixed_up = arrived[k, :, 1].reshape(rows, width)
        forward = dot(factor_v[...], mixed_in)
        backward = dot(factor_v[...], mixed_up)
        terms = forward * backward
        gains = kernel_v[k].astype(F32)
        weighted = (gains * forward).astype(BF16)
        pulled = (gains * backward).astype(BF16)
        back = dot(factor_t_v[...], pulled).reshape(n, PARTS, part, width)
        ahead = dot(factor_t_v[...], weighted).reshape(n, PARTS, part, width)
        for h in range(PARTS):
            spread[h, :, k] = jnp.concatenate([back[:, h], ahead[:, h]], axis=1).astype(BF16)
        peers(lambda target: back_copy(k, me, target).start())

        @pl.when(outer)
        def _():
            pair_terms[k] = terms.astype(BF16)
            outer_copy(k).start()

        @pl.when(inner)
        def _():
            own_terms[k] = terms

        second_acc[...] += dot_rows(mixed_in, pulled) + dot_rows(mixed_up, weighted)

        @pl.when(jnp.logical_and(inner, k >= 1))
        def _():
            make_pair(k - 1)

        @pl.when(jnp.logical_and(inner, k >= 2))
        def _():
            make_final(k - 2)

        return carry

    lax.fori_loop(0, chunks, transform, 0)
    for h in range(1, PARTS):
        peers(lambda target, h=h: late_copy(h, me, target).start())
    for h in range(PARTS):
        returned[h, me] = spread[h, me]

    second_terms[z] = jnp.sum(
        jnp.where(same_block, second_acc[...].reshape(shape), 0.0), axis=1
    )
    line_peers(lambda target: second_copy(z, target).start())

    @pl.when(inner)
    def _():
        make_pair(chunks - 1)
        if chunks >= 2:
            make_final(chunks - 2)

    for h in range(PARTS):
        first_acc[...] = jnp.zeros_like(first_acc)
        if h > 0:
            peers(lambda source, h=h: late_copy(h, source, me).wait_recv())

        def gather(k, carry, h=h):
            if h == 0:
                peers(lambda source: back_copy(k, source, me).wait_recv())
            both = returned[h, :, k].reshape(n * 2 * part, width)
            by_tokens = dot_rows(both, tokens_v[k]).reshape(n, 2, part, rows)
            by_cotangent = dot_rows(both, cotangent_v[k]).reshape(n, 2, part, rows)
            first_acc[...] += by_tokens[:, 0] + by_cotangent[:, 1]
            return carry

        lax.fori_loop(0, chunks, gather, 0)
        first_terms[h, z] = first_acc[...].reshape(n * part, rows).astype(BF16)
        line_peers(lambda target, h=h: first_copy(h, z, target).start())
        if h == 0:

            @pl.when(inner)
            def _():
                make_final(chunks - 1)

            line_peers(lambda source: second_copy(source, z).wait_recv())
            rest = jnp.sum(second_terms[...], axis=0) * factor_share
            pieces = []
            for _ in range(3):
                pieces.append(rest.astype(BF16))
                rest = rest - pieces[-1].astype(F32)
            for p in range(n):
                second_out[p] = sum(dot_rows(piece, picks[p]) for piece in reversed(pieces))

    stores = []
    for k in range(chunks):

        @pl.when(outer)
        def _():
            final_copy(k).wait_recv()

        stores.append(
            pltpu.make_async_copy(final_terms.at[k], kernel_out.at[:, pl.ds(k * width, width)], store_sem.at[k])
        )
        stores[-1].start()

    for h in range(PARTS):
        line_peers(lambda source, h=h: first_copy(h, source, z).wait_recv())
        total = jnp.sum(first_terms[h].astype(F32), axis=0) * factor_share
        first_out[:, h] = total.reshape(n, part, rows)

    for store in stores:
        store.wait()
    for k in range(chunks):
        peers(lambda target, k=k: out_copy(k, me, target).wait_send())
        peers(lambda target, k=k: back_copy(k, me, target).wait_send())

        @pl.when(outer)
        def _():
            outer_copy(k).wait_send()

        @pl.when(inner)
        def _():
            pair_copy(k).wait_send()
            final_copy(k).wait_send()

    line_peers(lambda target: second_copy(z, target).wait_send())
    for h in range(1, PARTS):
        peers(lambda target, h=h: late_copy(h, me, target).wait_send())
    for h in range(PARTS):
        line_peers(lambda target, h=h: first_copy(h, z, target).wait_send())


def fused(n, groups, tokens, cotangent, kernel, first_factor, second_factor):
    rows, channels = tokens.shape[1:]
    chunks = CHUNKS
    width = channels // chunks
    block = rows // n
    part = block // PARTS
    seq_share = 1.0 / math.sqrt(groups)
    factor_share = 1.0 / math.sqrt(2.0 * channels * groups)
    second = jnp.transpose(second_factor, (1, 2, 0))
    any_spec = pl.BlockSpec(memory_space=pl.ANY)
    vmem_spec = pl.BlockSpec(memory_space=pltpu.VMEM)
    dma = pltpu.SemaphoreType.DMA
    kernel_grad, first_grad, second_grad = pl.pallas_call(
        functools.partial(mixer_kernel, n, groups, chunks, seq_share, factor_share),
        out_shape=(
            jax.ShapeDtypeStruct((rows, channels), BF16),
            jax.ShapeDtypeStruct((n, PARTS, part, rows), F32),
            jax.ShapeDtypeStruct((n, n, block), F32),
        ),
        in_specs=[any_spec] * 4 + [vmem_spec],
        out_specs=(any_spec, vmem_spec, vmem_spec),
        scratch_shapes=[
            pltpu.VMEM((rows, rows), BF16),
            pltpu.VMEM((chunks, rows, width), BF16),
            pltpu.VMEM((chunks, rows, width), BF16),
            pltpu.VMEM((chunks, rows, width), BF16),
            pltpu.VMEM((rows, rows), BF16),
            pltpu.VMEM((rows, rows), BF16),
            pltpu.VMEM((chunks, n, 2, block, width), BF16),
            pltpu.VMEM((chunks, n, 2, block, width), BF16),
            pltpu.VMEM((PARTS, n, chunks, 2 * part, width), BF16),
            pltpu.VMEM((PARTS, n, chunks, 2 * part, width), BF16),
            pltpu.VMEM((chunks, rows, width), F32),
            pltpu.VMEM((chunks, rows, width), BF16),
            pltpu.VMEM((chunks, rows, width), BF16),
            pltpu.VMEM((chunks, rows, width), BF16),
            pltpu.VMEM((chunks, rows, width), BF16),
            pltpu.VMEM((rows, rows), F32),
            pltpu.VMEM((groups, n, rows), F32),
            pltpu.VMEM((n, part, rows), F32),
            pltpu.VMEM((PARTS, groups, n * part, rows), BF16),
            dma((chunks, 3)),
            dma,
            dma((chunks,)),
            dma((chunks, n)),
            dma((chunks, n)),
            dma((chunks, n)),
            dma((chunks, n)),
            dma((PARTS, n)),
            dma((PARTS, n)),
            dma((chunks,)),
            dma((chunks,)),
            dma((chunks,)),
            dma((chunks,)),
            dma((chunks,)),
            dma((chunks,)),
            dma((groups,)),
            dma((groups,)),
            dma((PARTS, groups)),
            dma((PARTS, groups)),
        ],
        compiler_params=pltpu.CompilerParams(
            collective_id=0, has_side_effects=True, vmem_limit_bytes=60 * 1024 * 1024
        ),
        cost_estimate=pl.CostEstimate(
            flops=16 * rows * rows * channels, bytes_accessed=8 * rows * channels, transcendentals=0
        ),
    )(tokens, cotangent, kernel, first_factor, second)
    second_grad = jnp.transpose(second_grad, (2, 0, 1))
    return kernel_grad, first_grad.reshape(1, rows, rows), second_grad


def separate(tokens, cotangent, kernel, first_factor, second_factor):
    local_rows = tokens.shape[1]
    channels = tokens.shape[2]
    column_blocks = second_factor.shape[0]
    mixed_in = jnp.einsum(
        "aqb,abc->aqc", first_factor, tokens, preferred_element_type=jnp.float32
    ).astype(jnp.bfloat16)
    mixed_up = jnp.einsum(
        "aqb,abc->aqc", first_factor, cotangent, preferred_element_type=jnp.float32
    ).astype(jnp.bfloat16)
    arrived_in = lax.all_to_all(mixed_in, "seq", split_axis=1, concat_axis=0, tiled=True)
    arrived_up = lax.all_to_all(mixed_up, "seq", split_axis=1, concat_axis=0, tiled=True)
    forward = jnp.einsum(
        "bpa,abc->bpc", second_factor, arrived_in, preferred_element_type=jnp.float32
    )
    backward = jnp.einsum(
        "bpa,abc->bpc", second_factor, arrived_up, preferred_element_type=jnp.float32
    )
    arrived_in, arrived_up, forward, backward = (arrived_in, arrived_up, forward, backward)
    kernel_local = kernel.reshape(column_blocks, -1, channels)
    kernel_grad = forward * backward
    weighted = (kernel_local * forward).astype(jnp.bfloat16)
    pulled = (kernel_local * backward).astype(jnp.bfloat16)
    second_grad = jnp.einsum(
        "bpc,abc->bpa", pulled, arrived_in, preferred_element_type=jnp.float32
    ) + jnp.einsum("bpc,abc->bpa", weighted, arrived_up, preferred_element_type=jnp.float32)
    spread = jnp.einsum(
        "bpa,bpc->abc", second_factor, weighted, preferred_element_type=jnp.float32
    ).astype(jnp.bfloat16)
    pulled_back = jnp.einsum(
        "bpa,bpc->abc", second_factor, pulled, preferred_element_type=jnp.float32
    ).astype(jnp.bfloat16)
    seq_share = 1.0 / math.sqrt(lax.axis_size("dp"))
    factor_share = 1.0 / math.sqrt(2.0 * channels * lax.axis_size("dp"))
    returned, returned_back = (
        lax.all_to_all(spread, "seq", split_axis=0, concat_axis=1, tiled=True),
        lax.all_to_all(pulled_back, "seq", split_axis=0, concat_axis=1, tiled=True),
    )
    first_grad = jnp.einsum(
        "aqc,abc->aqb", returned_back, tokens, preferred_element_type=jnp.float32
    ) + jnp.einsum("aqc,abc->aqb", returned, cotangent, preferred_element_type=jnp.float32)
    kernel_total, first_total, second_total = lax.psum((kernel_grad, first_grad, second_grad), "dp")
    kernel_out = (kernel_total * seq_share).astype(jnp.bfloat16)
    return (
        kernel_out.reshape(local_rows, channels),
        first_total * factor_share,
        second_total * factor_share,
    )


def shards(tokens, cotangent, kernel, first_factor, second_factor):
    n = lax.axis_size("seq")
    groups = lax.axis_size("dp")
    rows, channels = tokens.shape[1:]
    fits = (
        groups == 4
        and first_factor.shape[0] == 1
        and second_factor.shape[1] == n
        and second_factor.shape[0] == 8 * PARTS
        and n == 8
        and channels % (128 * CHUNKS) == 0
        and rows == n * second_factor.shape[0]
    )
    arguments = (tokens, cotangent, kernel, first_factor, second_factor)
    return fused(n, groups, *arguments) if fits else separate(*arguments)


def solution(mesh):
    in_specs = (
        P("dp", "seq", None),
        P("dp", "seq", None),
        P("seq", None),
        P("seq", None, None),
        P("seq", None, None),
    )
    out_specs = (P("seq", None), P("seq", None, None), P("seq", None, None))
    return jax.shard_map(shards, mesh=mesh, in_specs=in_specs, out_specs=out_specs, check_vma=False)
```

```python
import functools
import math

import jax
import jax.numpy as jnp
from jax import lax
from jax.experimental import pallas as pl
from jax.experimental.pallas import tpu as pltpu
from jax.sharding import PartitionSpec as P

MESH = pl.DeviceIdType.MESH
BF16 = jnp.bfloat16
F32 = jnp.float32
HALVES = 2
CHUNKS = 4


def dot(left, right):
    return jnp.dot(left, right, preferred_element_type=F32)


def dot_rows(left, right):
    return lax.dot_general(left, right, (((1,), (1,)), ((), ())), preferred_element_type=F32)


def flipped(index, mask):
    result = 0
    for bit in (1, 2, 4):
        own, flip = lax.rem(index // bit, 2), lax.rem(mask // bit, 2)
        result = result + bit * (own + flip - 2 * own * flip)
    return result


def mixer_kernel(
    n,
    groups,
    chunks,
    factor_share,
    tokens_ref,
    cotangent_ref,
    kernel_ref,
    first_ref,
    second_ref,
    kernel_out,
    first_out,
    second_out,
    first_v,
    tokens_v,
    cotangent_v,
    kernel_v,
    factor_v,
    factor_t_v,
    mixed,
    arrived,
    spread,
    returned,
    own_terms,
    outer_terms,
    pair_terms,
    other_terms,
    final_terms,
    second_acc,
    second_terms,
    first_acc,
    first_terms,
    first_in,
    first_done,
    load_sem,
    first_load_sem,
    store_sem,
    out_send,
    out_recv,
    back_send,
    back_recv,
    outer_send,
    outer_recv,
    pair_send,
    pair_recv,
    final_send,
    final_recv,
    second_send,
    second_recv,
    scatter_send,
    scatter_recv,
    gather_send,
    gather_recv,
):
    me = lax.axis_index("seq")
    z = lax.axis_index("dp")
    inner = jnp.logical_and(z >= 1, z <= 2)
    outer = jnp.logical_not(inner)
    rows = first_v.shape[0]
    width = tokens_v.shape[2]
    block = rows // n
    part = block // HALVES

    first_load = pltpu.make_async_copy(first_ref.at[0], first_v, first_load_sem)
    first_load.start()
    loads = []
    for k in range(chunks):
        columns = pl.ds(k * width, width)
        trio = [
            pltpu.make_async_copy(tokens_ref.at[0, :, columns], tokens_v.at[k], load_sem.at[k, 0]),
            pltpu.make_async_copy(cotangent_ref.at[0, :, columns], cotangent_v.at[k], load_sem.at[k, 1]),
            pltpu.make_async_copy(kernel_ref.at[:, columns], kernel_v.at[k], load_sem.at[k, 2]),
        ]
        trio[0].start()
        trio[1].start()
        loads.append(trio)
    for trio in loads:
        trio[2].start()

    barrier = pltpu.get_barrier_semaphore()
    for d in range(1, n):
        pl.semaphore_signal(barrier, inc=1, device_id={"seq": lax.rem(me + d, n)}, device_id_type=MESH)
    for d in range(1, groups):
        pl.semaphore_signal(barrier, inc=1, device_id={"dp": lax.rem(z + d, groups)}, device_id_type=MESH)

    shape = (n, block, rows)
    row_block = lax.broadcasted_iota(jnp.int32, shape, 1) * n
    column = lax.broadcasted_iota(jnp.int32, shape, 2)
    same_block = jnp.logical_and(column >= row_block, column < row_block + n)
    pick_block = lax.broadcasted_iota(jnp.int32, (block, rows), 0) * n
    pick_column = lax.broadcasted_iota(jnp.int32, (block, rows), 1)
    picks = [(pick_column == pick_block + p).astype(F32).astype(BF16) for p in range(n)]
    second = sum(dot(second_ref[p], picks[p]) for p in range(n))
    spread_factor = jnp.broadcast_to(second[:, None, :], shape)
    transposed = jnp.where(same_block, spread_factor, 0.0).reshape(rows, rows)
    factor_t_v[...] = transposed.astype(BF16)
    factor_v[...] = transposed.T.astype(BF16)
    second_acc[...] = jnp.zeros_like(second_acc)

    def out_copy(k, source, target):
        return pltpu.make_async_remote_copy(
            src_ref=mixed.at[k, target],
            dst_ref=arrived.at[k, source],
            send_sem=out_send.at[k, target],
            recv_sem=out_recv.at[k, source],
            device_id={"seq": target},
            device_id_type=MESH,
        )

    def back_copy(h, k, source, target):
        return pltpu.make_async_remote_copy(
            src_ref=spread.at[h, k, target],
            dst_ref=returned.at[h, k, source],
            send_sem=back_send.at[h, k, target],
            recv_sem=back_recv.at[h, k, source],
            device_id={"seq": target},
            device_id_type=MESH,
        )

    def line_copy(src, dst, send, recv, target):
        return pltpu.make_async_remote_copy(
            src_ref=src,
            dst_ref=dst,
            send_sem=send,
            recv_sem=recv,
            device_id={"dp": target},
            device_id_type=MESH,
        )

    inner_partner = 1 + z // 3
    outer_partner = (z - 1) * 3
    other_inner = 3 - z

    def outer_copy(k):
        return line_copy(pair_terms.at[k], outer_terms.at[k], outer_send.at[k], outer_recv.at[k], inner_partner)

    def pair_copy(k):
        return line_copy(pair_terms.at[k], other_terms.at[k], pair_send.at[k], pair_recv.at[k], other_inner)

    def final_copy(k):
        return line_copy(final_terms.at[k], final_terms.at[k], final_send.at[k], final_recv.at[k], outer_partner)

    def second_copy(source, target):
        return line_copy(
            second_terms.at[source], second_terms.at[source], second_send.at[target], second_recv.at[source], target
        )

    def scatter_copy(h, source, target):
        return line_copy(
            first_terms.at[h, target],
            first_in.at[h, source],
            scatter_send.at[h, target],
            scatter_recv.at[h, source],
            target,
        )

    def gather_copy(h, source, target):
        return line_copy(
            first_done.at[h, source],
            first_done.at[h, source],
            gather_send.at[h, target],
            gather_recv.at[h, source],
            target,
        )

    def peers(action):
        def step(i, carry):
            action(flipped(me, 1 + lax.rem(2 * i + 1, n - 1)))
            return carry

        lax.fori_loop(0, n - 1, step, 0)

    def line_peers(action):
        for d in range(1, groups):
            action(lax.rem(z + d, groups))

    first_load.wait()
    for k in range(chunks):
        loads[k][0].wait()
        loads[k][1].wait()
        mixed[k, :, 0] = dot(first_v[...], tokens_v[k]).astype(BF16).reshape(n, block, width)
        mixed[k, :, 1] = dot(first_v[...], cotangent_v[k]).astype(BF16).reshape(n, block, width)
        if k == 0:
            pl.semaphore_wait(barrier, n + groups - 2)
        peers(lambda target, k=k: out_copy(k, me, target).start())
        arrived[k, me] = mixed[k, me]
    for trio in loads:
        trio[2].wait()

    def make_pair(k):
        outer_copy(k).wait_recv()
        pair_terms[k] = (own_terms[k] + outer_terms[k].astype(F32)).astype(BF16)
        pair_copy(k).start()

    def make_final(k):
        pair_copy(k).wait_recv()
        total = pair_terms[k].astype(F32) + other_terms[k].astype(F32)
        final_terms[k] = total.astype(BF16)
        final_copy(k).start()

    def transform(k, carry):
        peers(lambda source: out_copy(k, source, me).wait_recv())
        mixed_in = arrived[k, :, 0].reshape(rows, width)
        mixed_up = arrived[k, :, 1].reshape(rows, width)
        forward = dot(factor_v[...], mixed_in)
        backward = dot(factor_v[...], mixed_up)
        terms = forward * backward
        gains = kernel_v[k].astype(F32)
        weighted = (gains * forward).astype(BF16)
        pulled = (gains * backward).astype(BF16)

        @pl.when(outer)
        def _():
            pair_terms[k] = terms.astype(BF16)
            outer_copy(k).start()

        @pl.when(inner)
        def _():
            own_terms[k] = terms

        back = dot(factor_t_v[...], pulled).astype(BF16).reshape(n, HALVES, part, width)
        ahead = dot(factor_t_v[...], weighted).astype(BF16).reshape(n, HALVES, part, width)
        for h in range(HALVES):
            spread[h, k, :, 0] = back[:, h]
            spread[h, k, :, 1] = ahead[:, h]
        peers(lambda target: back_copy(0, k, me, target).start())
        for h in range(HALVES):
            returned[h, k, me] = spread[h, k, me]
        second_acc[...] += dot_rows(mixed_in, pulled) + dot_rows(mixed_up, weighted)

        @pl.when(jnp.logical_and(inner, k >= 1))
        def _():
            make_pair(k - 1)

        @pl.when(jnp.logical_and(inner, k >= 2))
        def _():
            make_final(k - 2)

        return carry

    lax.fori_loop(0, chunks, transform, 0)
    second_terms[z] = jnp.sum(
        jnp.where(same_block, second_acc[...].reshape(shape), 0.0), axis=1
    )
    line_peers(lambda target: second_copy(z, target).start())

    @pl.when(inner)
    def _():
        make_pair(chunks - 1)
        if chunks >= 2:
            make_final(chunks - 2)

    first_acc[...] = jnp.zeros_like(first_acc)

    def gather(h):
        def step(k, carry):
            peers(lambda source: back_copy(h, k, source, me).wait_recv())
            if h + 1 < HALVES:
                peers(lambda target: back_copy(h + 1, k, me, target).start())
            back = returned[h, k, :, 0].reshape(n * part, width)
            ahead = returned[h, k, :, 1].reshape(n * part, width)
            first_acc[h] += dot_rows(back, tokens_v[k]) + dot_rows(ahead, cotangent_v[k])
            return carry

        return step

    def scatter(h):
        first_terms[h] = first_acc[h].astype(BF16).reshape(groups, n * part // groups, rows)
        line_peers(lambda target: scatter_copy(h, z, target).start())

    def combine(h):
        line_peers(lambda source: scatter_copy(h, source, z).wait_recv())
        total = first_terms[h, z].astype(F32)
        for d in range(1, groups):
            total = total + first_in[h, lax.rem(z + d, groups)].astype(F32)
        first_done[h, z] = total.astype(BF16)
        line_peers(lambda target: gather_copy(h, z, target).start())

    lax.fori_loop(0, chunks, gather(0), 0)

    @pl.when(inner)
    def _():
        make_final(chunks - 1)

    scatter(0)
    line_peers(lambda source: second_copy(source, z).wait_recv())
    rest = jnp.sum(second_terms[...], axis=0) * factor_share
    pieces = []
    for _ in range(3):
        pieces.append(rest.astype(BF16))
        rest = rest - pieces[-1].astype(F32)
    for p in range(n):
        second_out[p] = sum(dot_rows(piece, picks[p]) for piece in reversed(pieces))
    lax.fori_loop(0, chunks // 2, gather(1), 0)
    combine(0)
    lax.fori_loop(chunks // 2, chunks, gather(1), 0)
    scatter(1)

    stores = []
    for k in range(chunks):

        @pl.when(outer)
        def _():
            final_copy(k).wait_recv()

        stores.append(
            pltpu.make_async_copy(final_terms.at[k], kernel_out.at[:, pl.ds(k * width, width)], store_sem.at[k])
        )
        stores[-1].start()

    combine(1)
    for h in range(HALVES):
        line_peers(lambda source, h=h: gather_copy(h, source, z).wait_recv())
        first_out[:, h] = first_done[h].astype(F32).reshape(n, part, rows)

    for store in stores:
        store.wait()
    for k in range(chunks):
        peers(lambda target, k=k: out_copy(k, me, target).wait_send())
        for h in range(HALVES):
            peers(lambda target, h=h, k=k: back_copy(h, k, me, target).wait_send())

        @pl.when(outer)
        def _():
            outer_copy(k).wait_send()

        @pl.when(inner)
        def _():
            pair_copy(k).wait_send()
            final_copy(k).wait_send()

    line_peers(lambda target: second_copy(z, target).wait_send())
    for h in range(HALVES):
        line_peers(lambda target, h=h: scatter_copy(h, z, target).wait_send())
        line_peers(lambda target, h=h: gather_copy(h, z, target).wait_send())


def fused(n, groups, tokens, cotangent, kernel, first_factor, second_factor):
    rows, channels = tokens.shape[1:]
    chunks = CHUNKS
    width = channels // chunks
    block = rows // n
    part = block // HALVES
    seq_share = 1.0 / math.sqrt(groups)
    factor_share = 1.0 / math.sqrt(2.0 * channels * groups)
    second = jnp.transpose(second_factor, (1, 2, 0))
    any_spec = pl.BlockSpec(memory_space=pl.ANY)
    vmem_spec = pl.BlockSpec(memory_space=pltpu.VMEM)
    dma = pltpu.SemaphoreType.DMA
    kernel_grad, first_grad, second_grad = pl.pallas_call(
        functools.partial(mixer_kernel, n, groups, chunks, factor_share),
        out_shape=(
            jax.ShapeDtypeStruct((rows, channels), BF16),
            jax.ShapeDtypeStruct((n, HALVES, part, rows), F32),
            jax.ShapeDtypeStruct((n, n, block), F32),
        ),
        in_specs=[any_spec] * 4 + [vmem_spec],
        out_specs=(any_spec, vmem_spec, vmem_spec),
        scratch_shapes=[
            pltpu.VMEM((rows, rows), BF16),
            pltpu.VMEM((chunks, rows, width), BF16),
            pltpu.VMEM((chunks, rows, width), BF16),
            pltpu.VMEM((chunks, rows, width), BF16),
            pltpu.VMEM((rows, rows), BF16),
            pltpu.VMEM((rows, rows), BF16),
            pltpu.VMEM((chunks, n, 2, block, width), BF16),
            pltpu.VMEM((chunks, n, 2, block, width), BF16),
            pltpu.VMEM((HALVES, chunks, n, 2, part, width), BF16),
            pltpu.VMEM((HALVES, chunks, n, 2, part, width), BF16),
            pltpu.VMEM((chunks, rows, width), F32),
            pltpu.VMEM((chunks, rows, width), BF16),
            pltpu.VMEM((chunks, rows, width), BF16),
            pltpu.VMEM((chunks, rows, width), BF16),
            pltpu.VMEM((chunks, rows, width), BF16),
            pltpu.VMEM((rows, rows), F32),
            pltpu.VMEM((groups, n, rows), F32),
            pltpu.VMEM((HALVES, n * part, rows), F32),
            pltpu.VMEM((HALVES, groups, n * part // groups, rows), BF16),
            pltpu.VMEM((HALVES, groups, n * part // groups, rows), BF16),
            pltpu.VMEM((HALVES, groups, n * part // groups, rows), BF16),
            dma((chunks, 3)),
            dma,
            dma((chunks,)),
            dma((chunks, n)),
            dma((chunks, n)),
            dma((HALVES, chunks, n)),
            dma((HALVES, chunks, n)),
            dma((chunks,)),
            dma((chunks,)),
            dma((chunks,)),
            dma((chunks,)),
            dma((chunks,)),
            dma((chunks,)),
            dma((groups,)),
            dma((groups,)),
            dma((HALVES, groups)),
            dma((HALVES, groups)),
            dma((HALVES, groups)),
            dma((HALVES, groups)),
        ],
        compiler_params=pltpu.CompilerParams(
            collective_id=0, has_side_effects=True, vmem_limit_bytes=60 * 1024 * 1024
        ),
        cost_estimate=pl.CostEstimate(
            flops=16 * rows * rows * channels, bytes_accessed=8 * rows * channels, transcendentals=0
        ),
    )(tokens, cotangent, kernel, first_factor, second)
    second_grad = jnp.transpose(second_grad, (2, 0, 1))
    kernel_grad = (kernel_grad.astype(F32) * seq_share).astype(BF16)
    return kernel_grad, first_grad.reshape(1, rows, rows) * factor_share, second_grad


def separate(tokens, cotangent, kernel, first_factor, second_factor):
    local_rows = tokens.shape[1]
    channels = tokens.shape[2]
    column_blocks = second_factor.shape[0]
    mixed_in = jnp.einsum(
        "aqb,abc->aqc", first_factor, tokens, preferred_element_type=jnp.float32
    ).astype(jnp.bfloat16)
    mixed_up = jnp.einsum(
        "aqb,abc->aqc", first_factor, cotangent, preferred_element_type=jnp.float32
    ).astype(jnp.bfloat16)
    arrived_in = lax.all_to_all(mixed_in, "seq", split_axis=1, concat_axis=0, tiled=True)
    arrived_up = lax.all_to_all(mixed_up, "seq", split_axis=1, concat_axis=0, tiled=True)
    forward = jnp.einsum(
        "bpa,abc->bpc", second_factor, arrived_in, preferred_element_type=jnp.float32
    )
    backward = jnp.einsum(
        "bpa,abc->bpc", second_factor, arrived_up, preferred_element_type=jnp.float32
    )
    arrived_in, arrived_up, forward, backward = (arrived_in, arrived_up, forward, backward)
    kernel_local = kernel.reshape(column_blocks, -1, channels)
    kernel_grad = forward * backward
    weighted = (kernel_local * forward).astype(jnp.bfloat16)
    pulled = (kernel_local * backward).astype(jnp.bfloat16)
    second_grad = jnp.einsum(
        "bpc,abc->bpa", pulled, arrived_in, preferred_element_type=jnp.float32
    ) + jnp.einsum("bpc,abc->bpa", weighted, arrived_up, preferred_element_type=jnp.float32)
    spread = jnp.einsum(
        "bpa,bpc->abc", second_factor, weighted, preferred_element_type=jnp.float32
    ).astype(jnp.bfloat16)
    pulled_back = jnp.einsum(
        "bpa,bpc->abc", second_factor, pulled, preferred_element_type=jnp.float32
    ).astype(jnp.bfloat16)
    seq_share = 1.0 / math.sqrt(lax.axis_size("dp"))
    factor_share = 1.0 / math.sqrt(2.0 * channels * lax.axis_size("dp"))
    returned, returned_back = (
        lax.all_to_all(spread, "seq", split_axis=0, concat_axis=1, tiled=True),
        lax.all_to_all(pulled_back, "seq", split_axis=0, concat_axis=1, tiled=True),
    )
    first_grad = jnp.einsum(
        "aqc,abc->aqb", returned_back, tokens, preferred_element_type=jnp.float32
    ) + jnp.einsum("aqc,abc->aqb", returned, cotangent, preferred_element_type=jnp.float32)
    kernel_total, first_total, second_total = lax.psum((kernel_grad, first_grad, second_grad), "dp")
    kernel_out = (kernel_total * seq_share).astype(jnp.bfloat16)
    return (
        kernel_out.reshape(local_rows, channels),
        first_total * factor_share,
        second_total * factor_share,
    )


def shards(tokens, cotangent, kernel, first_factor, second_factor):
    n = lax.axis_size("seq")
    groups = lax.axis_size("dp")
    rows, channels = tokens.shape[1:]
    fits = (
        groups == 4
        and first_factor.shape[0] == 1
        and second_factor.shape[1] == n
        and second_factor.shape[0] == 16 * HALVES
        and n == 8
        and channels % (128 * CHUNKS) == 0
        and rows == n * second_factor.shape[0]
    )
    arguments = (tokens, cotangent, kernel, first_factor, second_factor)
    return fused(n, groups, *arguments) if fits else separate(*arguments)


def solution(mesh):
    in_specs = (
        P("dp", "seq", None),
        P("dp", "seq", None),
        P("seq", None),
        P("seq", None, None),
        P("seq", None, None),
    )
    out_specs = (P("seq", None), P("seq", None, None), P("seq", None, None))
    return jax.shard_map(shards, mesh=mesh, in_specs=in_specs, out_specs=out_specs, check_vma=False)
```

```python
import functools
import math

import jax
import jax.numpy as jnp
from jax import lax
from jax.experimental import pallas as pl
from jax.experimental.pallas import tpu as pltpu
from jax.sharding import PartitionSpec as P

MESH = pl.DeviceIdType.MESH
BF16 = jnp.bfloat16
F32 = jnp.float32
HALVES = 2
CHUNKS = 4


def dot(left, right):
    return jnp.dot(left, right, preferred_element_type=F32)


def dot_rows(left, right):
    return lax.dot_general(left, right, (((1,), (1,)), ((), ())), preferred_element_type=F32)


def partner(index, mask):
    core, x, y = lax.rem(index, 2), lax.rem(index // 2, 2), index // 4
    flip_core, low, high = lax.rem(mask, 2), lax.rem(mask // 2, 2), mask // 4
    flip_x = low * (1 - core) + high * core
    flip_y = high * (1 - core) + low * core
    flip = lambda own, by: own + by - 2 * own * by
    return (flip(y, flip_y) * 2 + flip(x, flip_x)) * 2 + flip(core, flip_core)


def mixer_kernel(
    n,
    groups,
    chunks,
    seq_share,
    factor_share,
    tokens_ref,
    cotangent_ref,
    kernel_ref,
    first_ref,
    second_ref,
    kernel_out,
    first_out,
    second_out,
    first_v,
    tokens_v,
    cotangent_v,
    kernel_v,
    factor_v,
    factor_t_v,
    mixed,
    arrived,
    spread,
    returned,
    own_terms,
    outer_terms,
    pair_terms,
    other_terms,
    final_terms,
    second_acc,
    second_terms,
    first_acc,
    first_terms,
    first_in,
    first_done,
    load_sem,
    first_load_sem,
    store_sem,
    out_send,
    out_recv,
    back_send,
    back_recv,
    outer_send,
    outer_recv,
    pair_send,
    pair_recv,
    final_send,
    final_recv,
    second_send,
    second_recv,
    scatter_send,
    scatter_recv,
    gather_send,
    gather_recv,
):
    me = lax.axis_index("seq")
    z = lax.axis_index("dp")
    inner = jnp.logical_and(z >= 1, z <= 2)
    outer = jnp.logical_not(inner)
    rows = first_v.shape[0]
    width = tokens_v.shape[2]
    block = rows // n
    part = block // HALVES

    first_load = pltpu.make_async_copy(first_ref.at[0], first_v, first_load_sem)
    first_load.start()
    loads = []
    for k in range(chunks):
        columns = pl.ds(k * width, width)
        trio = [
            pltpu.make_async_copy(tokens_ref.at[0, :, columns], tokens_v.at[k], load_sem.at[k, 0]),
            pltpu.make_async_copy(cotangent_ref.at[0, :, columns], cotangent_v.at[k], load_sem.at[k, 1]),
            pltpu.make_async_copy(kernel_ref.at[:, columns], kernel_v.at[k], load_sem.at[k, 2]),
        ]
        trio[0].start()
        trio[1].start()
        loads.append(trio)
    for trio in loads:
        trio[2].start()

    barrier = pltpu.get_barrier_semaphore()
    for d in range(1, n):
        pl.semaphore_signal(barrier, inc=1, device_id={"seq": lax.rem(me + d, n)}, device_id_type=MESH)
    for d in range(1, groups):
        pl.semaphore_signal(barrier, inc=1, device_id={"dp": lax.rem(z + d, groups)}, device_id_type=MESH)

    shape = (n, block, rows)
    row_block = lax.broadcasted_iota(jnp.int32, shape, 1) * n
    column = lax.broadcasted_iota(jnp.int32, shape, 2)
    same_block = jnp.logical_and(column >= row_block, column < row_block + n)
    pick_block = lax.broadcasted_iota(jnp.int32, (block, rows), 0) * n
    pick_column = lax.broadcasted_iota(jnp.int32, (block, rows), 1)
    picks = [(pick_column == pick_block + p).astype(F32).astype(BF16) for p in range(n)]
    second = sum(dot(second_ref[p], picks[p]) for p in range(n))
    spread_factor = jnp.broadcast_to(second[:, None, :], shape)
    transposed = jnp.where(same_block, spread_factor, 0.0).reshape(rows, rows)
    factor_t_v[...] = transposed.astype(BF16)
    factor_v[...] = transposed.T.astype(BF16)
    second_acc[...] = jnp.zeros_like(second_acc)

    def out_copy(k, source, target):
        return pltpu.make_async_remote_copy(
            src_ref=mixed.at[k, target],
            dst_ref=arrived.at[k, source],
            send_sem=out_send.at[k, target],
            recv_sem=out_recv.at[k, source],
            device_id={"seq": target},
            device_id_type=MESH,
        )

    def back_copy(h, k, source, target):
        return pltpu.make_async_remote_copy(
            src_ref=spread.at[h, k, target],
            dst_ref=returned.at[h, k, source],
            send_sem=back_send.at[h, k, target],
            recv_sem=back_recv.at[h, k, source],
            device_id={"seq": target},
            device_id_type=MESH,
        )

    def line_copy(src, dst, send, recv, target):
        return pltpu.make_async_remote_copy(
            src_ref=src,
            dst_ref=dst,
            send_sem=send,
            recv_sem=recv,
            device_id={"dp": target},
            device_id_type=MESH,
        )

    inner_partner = 1 + z // 3
    outer_partner = (z - 1) * 3
    other_inner = 3 - z

    def outer_copy(k):
        return line_copy(pair_terms.at[k], outer_terms.at[k], outer_send.at[k], outer_recv.at[k], inner_partner)

    def pair_copy(k):
        return line_copy(pair_terms.at[k], other_terms.at[k], pair_send.at[k], pair_recv.at[k], other_inner)

    def final_copy(k):
        return line_copy(final_terms.at[k], final_terms.at[k], final_send.at[k], final_recv.at[k], outer_partner)

    def second_copy(source, target):
        return line_copy(
            second_terms.at[source], second_terms.at[source], second_send.at[target], second_recv.at[source], target
        )

    def scatter_copy(h, source, target):
        return line_copy(
            first_terms.at[h, target],
            first_in.at[h, source],
            scatter_send.at[h, target],
            scatter_recv.at[h, source],
            target,
        )

    def gather_copy(h, source, target):
        return line_copy(
            first_done.at[h, source],
            first_done.at[h, source],
            gather_send.at[h, target],
            gather_recv.at[h, source],
            target,
        )

    def peers(action):
        def step(i, carry):
            action(partner(me, 1 + lax.rem(2 * i + 1, n - 1)))
            return carry

        lax.fori_loop(0, n - 1, step, 0)

    def line_peers(action):
        for d in range(1, groups):
            action(lax.rem(z + d, groups))

    first_load.wait()
    for k in range(chunks):
        loads[k][0].wait()
        loads[k][1].wait()
        mixed[k, :, 0] = dot(first_v[...], tokens_v[k]).astype(BF16).reshape(n, block, width)
        mixed[k, :, 1] = dot(first_v[...], cotangent_v[k]).astype(BF16).reshape(n, block, width)
        if k == 0:
            pl.semaphore_wait(barrier, n + groups - 2)
        peers(lambda target, k=k: out_copy(k, me, target).start())
        arrived[k, me] = mixed[k, me]
    for trio in loads:
        trio[2].wait()

    def make_pair(k):
        outer_copy(k).wait_recv()
        pair_terms[k] = (own_terms[k] + outer_terms[k].astype(F32)).astype(BF16)
        pair_copy(k).start()

    def make_final(k):
        pair_copy(k).wait_recv()
        total = pair_terms[k].astype(F32) + other_terms[k].astype(F32)
        final_terms[k] = (total * seq_share).astype(BF16)
        final_copy(k).start()

    def transform(k, carry):
        peers(lambda source: out_copy(k, source, me).wait_recv())
        mixed_in = arrived[k, :, 0].reshape(rows, width)
        mixed_up = arrived[k, :, 1].reshape(rows, width)
        forward = dot(factor_v[...], mixed_in)
        backward = dot(factor_v[...], mixed_up)
        terms = forward * backward
        gains = kernel_v[k].astype(F32)
        weighted = (gains * forward).astype(BF16)
        pulled = (gains * backward).astype(BF16)

        @pl.when(outer)
        def _():
            pair_terms[k] = terms.astype(BF16)
            outer_copy(k).start()

        @pl.when(inner)
        def _():
            own_terms[k] = terms

        back = dot(factor_t_v[...], pulled).astype(BF16).reshape(n, HALVES, part, width)
        ahead = dot(factor_t_v[...], weighted).astype(BF16).reshape(n, HALVES, part, width)
        for h in range(HALVES):
            spread[h, k, :, 0] = back[:, h]
            spread[h, k, :, 1] = ahead[:, h]
        peers(lambda target: back_copy(0, k, me, target).start())
        for h in range(HALVES):
            returned[h, k, me] = spread[h, k, me]
        second_acc[...] += dot_rows(mixed_in, pulled) + dot_rows(mixed_up, weighted)

        @pl.when(jnp.logical_and(inner, k >= 1))
        def _():
            make_pair(k - 1)

        @pl.when(jnp.logical_and(inner, k >= 2))
        def _():
            make_final(k - 2)

        return carry

    lax.fori_loop(0, chunks, transform, 0)
    for h in range(1, HALVES):
        for k in range(chunks):
            peers(lambda target, h=h, k=k: back_copy(h, k, me, target).start())
    second_terms[z] = jnp.sum(
        jnp.where(same_block, second_acc[...].reshape(shape), 0.0), axis=1
    )
    line_peers(lambda target: second_copy(z, target).start())

    @pl.when(inner)
    def _():
        make_pair(chunks - 1)
        if chunks >= 2:
            make_final(chunks - 2)

    first_acc[...] = jnp.zeros_like(first_acc)

    def gather(h):
        def step(k, carry):
            peers(lambda source: back_copy(h, k, source, me).wait_recv())
            back = returned[h, k, :, 0].reshape(n * part, width)
            ahead = returned[h, k, :, 1].reshape(n * part, width)
            first_acc[h] += dot_rows(back, tokens_v[k]) + dot_rows(ahead, cotangent_v[k])
            return carry

        return step

    def scatter(h):
        first_terms[h] = first_acc[h].astype(BF16).reshape(groups, n * part // groups, rows)
        line_peers(lambda target: scatter_copy(h, z, target).start())

    def combine(h):
        line_peers(lambda source: scatter_copy(h, source, z).wait_recv())
        total = first_terms[h, z].astype(F32)
        for d in range(1, groups):
            total = total + first_in[h, lax.rem(z + d, groups)].astype(F32)
        first_done[h, z] = total.astype(BF16)
        line_peers(lambda target: gather_copy(h, z, target).start())

    lax.fori_loop(0, chunks, gather(0), 0)

    @pl.when(inner)
    def _():
        make_final(chunks - 1)

    scatter(0)
    line_peers(lambda source: second_copy(source, z).wait_recv())
    rest = jnp.sum(second_terms[...], axis=0) * factor_share
    pieces = []
    for _ in range(3):
        pieces.append(rest.astype(BF16))
        rest = rest - pieces[-1].astype(F32)
    for p in range(n):
        second_out[p] = sum(dot_rows(piece, picks[p]) for piece in reversed(pieces))
    lax.fori_loop(0, chunks // 2, gather(1), 0)
    combine(0)
    lax.fori_loop(chunks // 2, chunks, gather(1), 0)
    scatter(1)

    stores = []
    for k in range(chunks):

        @pl.when(outer)
        def _():
            final_copy(k).wait_recv()

        stores.append(
            pltpu.make_async_copy(final_terms.at[k], kernel_out.at[:, pl.ds(k * width, width)], store_sem.at[k])
        )
        stores[-1].start()

    combine(1)
    for h in range(HALVES):
        line_peers(lambda source, h=h: gather_copy(h, source, z).wait_recv())
        total = first_done[h].astype(F32) * factor_share
        first_out[:, h] = total.reshape(n, part, rows)

    for store in stores:
        store.wait()
    for k in range(chunks):
        peers(lambda target, k=k: out_copy(k, me, target).wait_send())
        for h in range(HALVES):
            peers(lambda target, h=h, k=k: back_copy(h, k, me, target).wait_send())

        @pl.when(outer)
        def _():
            outer_copy(k).wait_send()

        @pl.when(inner)
        def _():
            pair_copy(k).wait_send()
            final_copy(k).wait_send()

    line_peers(lambda target: second_copy(z, target).wait_send())
    for h in range(HALVES):
        line_peers(lambda target, h=h: scatter_copy(h, z, target).wait_send())
        line_peers(lambda target, h=h: gather_copy(h, z, target).wait_send())


def copies_kernel(pieces, *refs):
    sources, results, sem = refs[: len(refs) // 2], refs[len(refs) // 2 : -1], refs[-1]
    copies = []
    for source, result in zip(sources, results, strict=True):
        parts = pieces if source.ndim == 2 else 1
        step = source.shape[0] // parts
        for part in range(parts):
            span = pl.ds(part * step, step)
            copies.append(pltpu.make_async_copy(source.at[span], result.at[span], sem.at[len(copies)]))
            copies[-1].start()
    for copy in copies:
        copy.wait()


def handed_on(*arrays):
    pieces = 4
    any_spec = pl.BlockSpec(memory_space=pl.ANY)
    return pl.pallas_call(
        functools.partial(copies_kernel, pieces),
        out_shape=tuple(jax.ShapeDtypeStruct(array.shape, array.dtype) for array in arrays),
        in_specs=[any_spec] * len(arrays),
        out_specs=(any_spec,) * len(arrays),
        scratch_shapes=[pltpu.SemaphoreType.DMA((pieces + len(arrays),))],
        compiler_params=pltpu.CompilerParams(vmem_limit_bytes=60 * 1024 * 1024),
    )(*arrays)


def fused(n, groups, tokens, cotangent, kernel, first_factor, second_factor):
    rows, channels = tokens.shape[1:]
    chunks = CHUNKS
    width = channels // chunks
    block = rows // n
    part = block // HALVES
    seq_share = 1.0 / math.sqrt(groups)
    factor_share = 1.0 / math.sqrt(2.0 * channels * groups)
    second = jnp.transpose(second_factor, (1, 2, 0))
    any_spec = pl.BlockSpec(memory_space=pl.ANY)
    vmem_spec = pl.BlockSpec(memory_space=pltpu.VMEM)
    dma = pltpu.SemaphoreType.DMA
    kernel_grad, first_grad, second_grad = pl.pallas_call(
        functools.partial(mixer_kernel, n, groups, chunks, seq_share, factor_share),
        out_shape=(
            jax.ShapeDtypeStruct((rows, channels), BF16),
            jax.ShapeDtypeStruct((n, HALVES, part, rows), F32),
            jax.ShapeDtypeStruct((n, n, block), F32),
        ),
        in_specs=[any_spec] * 4 + [vmem_spec],
        out_specs=(any_spec, vmem_spec, vmem_spec),
        scratch_shapes=[
            pltpu.VMEM((rows, rows), BF16),
            pltpu.VMEM((chunks, rows, width), BF16),
            pltpu.VMEM((chunks, rows, width), BF16),
            pltpu.VMEM((chunks, rows, width), BF16),
            pltpu.VMEM((rows, rows), BF16),
            pltpu.VMEM((rows, rows), BF16),
            pltpu.VMEM((chunks, n, 2, block, width), BF16),
            pltpu.VMEM((chunks, n, 2, block, width), BF16),
            pltpu.VMEM((HALVES, chunks, n, 2, part, width), BF16),
            pltpu.VMEM((HALVES, chunks, n, 2, part, width), BF16),
            pltpu.VMEM((chunks, rows, width), F32),
            pltpu.VMEM((chunks, rows, width), BF16),
            pltpu.VMEM((chunks, rows, width), BF16),
            pltpu.VMEM((chunks, rows, width), BF16),
            pltpu.VMEM((chunks, rows, width), BF16),
            pltpu.VMEM((rows, rows), F32),
            pltpu.VMEM((groups, n, rows), F32),
            pltpu.VMEM((HALVES, n * part, rows), F32),
            pltpu.VMEM((HALVES, groups, n * part // groups, rows), BF16),
            pltpu.VMEM((HALVES, groups, n * part // groups, rows), BF16),
            pltpu.VMEM((HALVES, groups, n * part // groups, rows), BF16),
            dma((chunks, 3)),
            dma,
            dma((chunks,)),
            dma((chunks, n)),
            dma((chunks, n)),
            dma((HALVES, chunks, n)),
            dma((HALVES, chunks, n)),
            dma((chunks,)),
            dma((chunks,)),
            dma((chunks,)),
            dma((chunks,)),
            dma((chunks,)),
            dma((chunks,)),
            dma((groups,)),
            dma((groups,)),
            dma((HALVES, groups)),
            dma((HALVES, groups)),
            dma((HALVES, groups)),
            dma((HALVES, groups)),
        ],
        compiler_params=pltpu.CompilerParams(
            collective_id=0, has_side_effects=True, vmem_limit_bytes=60 * 1024 * 1024
        ),
        cost_estimate=pl.CostEstimate(
            flops=16 * rows * rows * channels, bytes_accessed=8 * rows * channels, transcendentals=0
        ),
    )(tokens, cotangent, kernel, first_factor, second)
    kernel_grad, first_grad, second_grad = handed_on(kernel_grad, first_grad, second_grad)
    second_grad = jnp.transpose(second_grad, (2, 0, 1))
    return kernel_grad, first_grad.reshape(1, rows, rows), second_grad


def separate(tokens, cotangent, kernel, first_factor, second_factor):
    local_rows = tokens.shape[1]
    channels = tokens.shape[2]
    column_blocks = second_factor.shape[0]
    mixed_in = jnp.einsum(
        "aqb,abc->aqc", first_factor, tokens, preferred_element_type=jnp.float32
    ).astype(jnp.bfloat16)
    mixed_up = jnp.einsum(
        "aqb,abc->aqc", first_factor, cotangent, preferred_element_type=jnp.float32
    ).astype(jnp.bfloat16)
    arrived_in = lax.all_to_all(mixed_in, "seq", split_axis=1, concat_axis=0, tiled=True)
    arrived_up = lax.all_to_all(mixed_up, "seq", split_axis=1, concat_axis=0, tiled=True)
    forward = jnp.einsum(
        "bpa,abc->bpc", second_factor, arrived_in, preferred_element_type=jnp.float32
    )
    backward = jnp.einsum(
        "bpa,abc->bpc", second_factor, arrived_up, preferred_element_type=jnp.float32
    )
    arrived_in, arrived_up, forward, backward = (arrived_in, arrived_up, forward, backward)
    kernel_local = kernel.reshape(column_blocks, -1, channels)
    kernel_grad = forward * backward
    weighted = (kernel_local * forward).astype(jnp.bfloat16)
    pulled = (kernel_local * backward).astype(jnp.bfloat16)
    second_grad = jnp.einsum(
        "bpc,abc->bpa", pulled, arrived_in, preferred_element_type=jnp.float32
    ) + jnp.einsum("bpc,abc->bpa", weighted, arrived_up, preferred_element_type=jnp.float32)
    spread = jnp.einsum(
        "bpa,bpc->abc", second_factor, weighted, preferred_element_type=jnp.float32
    ).astype(jnp.bfloat16)
    pulled_back = jnp.einsum(
        "bpa,bpc->abc", second_factor, pulled, preferred_element_type=jnp.float32
    ).astype(jnp.bfloat16)
    seq_share = 1.0 / math.sqrt(lax.axis_size("dp"))
    factor_share = 1.0 / math.sqrt(2.0 * channels * lax.axis_size("dp"))
    returned, returned_back = (
        lax.all_to_all(spread, "seq", split_axis=0, concat_axis=1, tiled=True),
        lax.all_to_all(pulled_back, "seq", split_axis=0, concat_axis=1, tiled=True),
    )
    first_grad = jnp.einsum(
        "aqc,abc->aqb", returned_back, tokens, preferred_element_type=jnp.float32
    ) + jnp.einsum("aqc,abc->aqb", returned, cotangent, preferred_element_type=jnp.float32)
    kernel_total, first_total, second_total = lax.psum((kernel_grad, first_grad, second_grad), "dp")
    kernel_out = (kernel_total * seq_share).astype(jnp.bfloat16)
    return (
        kernel_out.reshape(local_rows, channels),
        first_total * factor_share,
        second_total * factor_share,
    )


def shards(tokens, cotangent, kernel, first_factor, second_factor):
    n = lax.axis_size("seq")
    groups = lax.axis_size("dp")
    rows, channels = tokens.shape[1:]
    fits = (
        groups == 4
        and first_factor.shape[0] == 1
        and second_factor.shape[1] == n
        and second_factor.shape[0] == 16 * HALVES
        and n == 8
        and channels % (128 * CHUNKS) == 0
        and rows == n * second_factor.shape[0]
    )
    arguments = (tokens, cotangent, kernel, first_factor, second_factor)
    return fused(n, groups, *arguments) if fits else separate(*arguments)


def solution(mesh):
    in_specs = (
        P("dp", "seq", None),
        P("dp", "seq", None),
        P("seq", None),
        P("seq", None, None),
        P("seq", None, None),
    )
    out_specs = (P("seq", None), P("seq", None, None), P("seq", None, None))
    return jax.shard_map(shards, mesh=mesh, in_specs=in_specs, out_specs=out_specs, check_vma=False)
```

```python
import functools
import math

import jax
import jax.numpy as jnp
from jax import lax
from jax.experimental import pallas as pl
from jax.experimental.pallas import tpu as pltpu
from jax.sharding import PartitionSpec as P

MESH = pl.DeviceIdType.MESH
BF16 = jnp.bfloat16
F32 = jnp.float32
PARTS = 4
CHUNKS = 4
AHEAD = 2


def dot(left, right):
    return jnp.dot(left, right, preferred_element_type=F32)


def dot_rows(left, right):
    return lax.dot_general(left, right, (((1,), (1,)), ((), ())), preferred_element_type=F32)


def partner(index, mask):
    core, x, y = lax.rem(index, 2), lax.rem(index // 2, 2), index // 4
    flip_core, low, high = lax.rem(mask, 2), lax.rem(mask // 2, 2), mask // 4
    flip_x = low * (1 - core) + high * core
    flip_y = high * (1 - core) + low * core
    flip = lambda own, by: own + by - 2 * own * by
    return (flip(y, flip_y) * 2 + flip(x, flip_x)) * 2 + flip(core, flip_core)


def mixer_kernel(
    n,
    groups,
    chunks,
    seq_share,
    factor_share,
    tokens_ref,
    cotangent_ref,
    kernel_ref,
    first_ref,
    second_ref,
    kernel_out,
    first_out,
    second_out,
    first_v,
    tokens_v,
    cotangent_v,
    kernel_v,
    factor_v,
    factor_t_v,
    mixed,
    arrived,
    spread,
    returned,
    own_terms,
    outer_terms,
    pair_terms,
    other_terms,
    final_terms,
    second_acc,
    second_terms,
    first_acc,
    first_terms,
    load_sem,
    first_load_sem,
    store_sem,
    out_send,
    out_recv,
    back_send,
    back_recv,
    late_send,
    late_recv,
    outer_send,
    outer_recv,
    pair_send,
    pair_recv,
    final_send,
    final_recv,
    second_send,
    second_recv,
    first_send,
    first_recv,
):
    me = lax.axis_index("seq")
    z = lax.axis_index("dp")
    inner = jnp.logical_and(z >= 1, z <= 2)
    outer = jnp.logical_not(inner)
    rows = first_v.shape[0]
    width = tokens_v.shape[2]
    block = rows // n
    part = block // PARTS

    first_load = pltpu.make_async_copy(first_ref.at[0], first_v, first_load_sem)
    first_load.start()
    loads = []
    for k in range(chunks):
        columns = pl.ds(k * width, width)
        trio = [
            pltpu.make_async_copy(tokens_ref.at[0, :, columns], tokens_v.at[k], load_sem.at[k, 0]),
            pltpu.make_async_copy(cotangent_ref.at[0, :, columns], cotangent_v.at[k], load_sem.at[k, 1]),
            pltpu.make_async_copy(kernel_ref.at[:, columns], kernel_v.at[k], load_sem.at[k, 2]),
        ]
        trio[0].start()
        trio[1].start()
        loads.append(trio)
    for trio in loads:
        trio[2].start()

    barrier = pltpu.get_barrier_semaphore()
    for d in range(1, n):
        pl.semaphore_signal(barrier, inc=1, device_id={"seq": lax.rem(me + d, n)}, device_id_type=MESH)
    for d in range(1, groups):
        pl.semaphore_signal(barrier, inc=1, device_id={"dp": lax.rem(z + d, groups)}, device_id_type=MESH)

    shape = (n, block, rows)
    row_block = lax.broadcasted_iota(jnp.int32, shape, 1) * n
    column = lax.broadcasted_iota(jnp.int32, shape, 2)
    same_block = jnp.logical_and(column >= row_block, column < row_block + n)
    pick_block = lax.broadcasted_iota(jnp.int32, (block, rows), 0) * n
    pick_column = lax.broadcasted_iota(jnp.int32, (block, rows), 1)
    picks = [(pick_column == pick_block + p).astype(F32).astype(BF16) for p in range(n)]
    second = sum(dot(second_ref[p], picks[p]) for p in range(n))
    spread_factor = jnp.broadcast_to(second[:, None, :], shape)
    transposed = jnp.where(same_block, spread_factor, 0.0).reshape(rows, rows)
    factor_t_v[...] = transposed.astype(BF16)
    factor_v[...] = transposed.T.astype(BF16)
    second_acc[...] = jnp.zeros_like(second_acc)

    def out_copy(k, source, target):
        return pltpu.make_async_remote_copy(
            src_ref=mixed.at[k, target],
            dst_ref=arrived.at[k, source],
            send_sem=out_send.at[k, target],
            recv_sem=out_recv.at[k, source],
            device_id={"seq": target},
            device_id_type=MESH,
        )

    def back_copy(k, source, target):
        return pltpu.make_async_remote_copy(
            src_ref=spread.at[0, target, k],
            dst_ref=returned.at[0, source, k],
            send_sem=back_send.at[k, target],
            recv_sem=back_recv.at[k, source],
            device_id={"seq": target},
            device_id_type=MESH,
        )

    def late_copy(h, source, target):
        return pltpu.make_async_remote_copy(
            src_ref=spread.at[h, target],
            dst_ref=returned.at[h, source],
            send_sem=late_send.at[h, target],
            recv_sem=late_recv.at[h, source],
            device_id={"seq": target},
            device_id_type=MESH,
        )

    def line_copy(src, dst, send, recv, target):
        return pltpu.make_async_remote_copy(
            src_ref=src,
            dst_ref=dst,
            send_sem=send,
            recv_sem=recv,
            device_id={"dp": target},
            device_id_type=MESH,
        )

    inner_partner = 1 + z // 3
    outer_partner = (z - 1) * 3
    other_inner = 3 - z

    def outer_copy(k):
        return line_copy(pair_terms.at[k], outer_terms.at[k], outer_send.at[k], outer_recv.at[k], inner_partner)

    def pair_copy(k):
        return line_copy(pair_terms.at[k], other_terms.at[k], pair_send.at[k], pair_recv.at[k], other_inner)

    def final_copy(k):
        return line_copy(final_terms.at[k], final_terms.at[k], final_send.at[k], final_recv.at[k], outer_partner)

    def second_copy(source, target):
        return line_copy(
            second_terms.at[source], second_terms.at[source], second_send.at[target], second_recv.at[source], target
        )

    def first_copy(h, source, target):
        return line_copy(
            first_terms.at[h, source], first_terms.at[h, source], first_send.at[h, target], first_recv.at[h, source], target
        )

    def peers(action):
        def step(i, carry):
            action(partner(me, 1 + lax.rem(2 * i + 1, n - 1)))
            return carry

        lax.fori_loop(0, n - 1, step, 0)

    def line_peers(action):
        for d in range(1, groups):
            action(lax.rem(z + d, groups))

    first_load.wait()
    for k in range(chunks):
        loads[k][0].wait()
        loads[k][1].wait()
        mixed[k, :, 0] = dot(first_v[...], tokens_v[k]).astype(BF16).reshape(n, block, width)
        mixed[k, :, 1] = dot(first_v[...], cotangent_v[k]).astype(BF16).reshape(n, block, width)
        if k == 0:
            pl.semaphore_wait(barrier, n + groups - 2)
        if k < AHEAD:
            peers(lambda target, k=k: out_copy(k, me, target).start())
        arrived[k, me] = mixed[k, me]
    for trio in loads:
        trio[2].wait()

    def make_pair(k):
        outer_copy(k).wait_recv()
        pair_terms[k] = (own_terms[k] + outer_terms[k].astype(F32)).astype(BF16)
        pair_copy(k).start()

    def make_final(k):
        pair_copy(k).wait_recv()
        total = pair_terms[k].astype(F32) + other_terms[k].astype(F32)
        final_terms[k] = (total * seq_share).astype(BF16)
        final_copy(k).start()

    def transform(k, carry):
        peers(lambda source: out_copy(k, source, me).wait_recv())

        @pl.when(k + AHEAD < chunks)
        def _():
            peers(lambda target: out_copy(k + AHEAD, me, target).start())

        mixed_in = arrived[k, :, 0].reshape(rows, width)
        mixed_up = arrived[k, :, 1].reshape(rows, width)
        forward = dot(factor_v[...], mixed_in)
        backward = dot(factor_v[...], mixed_up)
        terms = forward * backward
        gains = kernel_v[k].astype(F32)
        weighted = (gains * forward).astype(BF16)
        pulled = (gains * backward).astype(BF16)
        back = dot(factor_t_v[...], pulled).reshape(n, PARTS, part, width)
        ahead = dot(factor_t_v[...], weighted).reshape(n, PARTS, part, width)
        for h in range(PARTS):
            spread[h, :, k] = jnp.concatenate([back[:, h], ahead[:, h]], axis=1).astype(BF16)
        peers(lambda target: back_copy(k, me, target).start())

        @pl.when(outer)
        def _():
            pair_terms[k] = terms.astype(BF16)
            outer_copy(k).start()

        @pl.when(inner)
        def _():
            own_terms[k] = terms

        second_acc[...] += dot_rows(mixed_in, pulled) + dot_rows(mixed_up, weighted)

        @pl.when(jnp.logical_and(inner, k >= 2))
        def _():
            make_pair(k - 2)

        @pl.when(jnp.logical_and(inner, k >= 3))
        def _():
            make_final(k - 3)

        return carry

    lax.fori_loop(0, chunks, transform, 0)
    for h in range(1, PARTS):
        peers(lambda target, h=h: late_copy(h, me, target).start())
    for h in range(PARTS):
        returned[h, me] = spread[h, me]

    second_terms[z] = jnp.sum(
        jnp.where(same_block, second_acc[...].reshape(shape), 0.0), axis=1
    )
    line_peers(lambda target: second_copy(z, target).start())

    @pl.when(inner)
    def _():
        make_pair(chunks - 2)
        make_final(chunks - 3)

    for h in range(PARTS):
        first_acc[...] = jnp.zeros_like(first_acc)
        if h > 0:
            peers(lambda source, h=h: late_copy(h, source, me).wait_recv())

        def gather(k, carry, h=h):
            if h == 0:
                peers(lambda source: back_copy(k, source, me).wait_recv())
            both = returned[h, :, k].reshape(n * 2 * part, width)
            by_tokens = dot_rows(both, tokens_v[k]).reshape(n, 2, part, rows)
            by_cotangent = dot_rows(both, cotangent_v[k]).reshape(n, 2, part, rows)
            first_acc[...] += by_tokens[:, 0] + by_cotangent[:, 1]
            return carry

        lax.fori_loop(0, chunks // 2, gather, 0)
        if h == 0:

            @pl.when(inner)
            def _():
                make_pair(chunks - 1)
                make_final(chunks - 2)

        lax.fori_loop(chunks // 2, chunks, gather, 0)
        first_terms[h, z] = first_acc[...].reshape(n * part, rows).astype(BF16)
        line_peers(lambda target, h=h: first_copy(h, z, target).start())
        if h == 0:

            @pl.when(inner)
            def _():
                make_final(chunks - 1)

            line_peers(lambda source: second_copy(source, z).wait_recv())
            rest = jnp.sum(second_terms[...], axis=0) * factor_share
            pieces = []
            for _ in range(3):
                pieces.append(rest.astype(BF16))
                rest = rest - pieces[-1].astype(F32)
            for p in range(n):
                second_out[p] = sum(dot_rows(piece, picks[p]) for piece in reversed(pieces))

    stores = []
    for k in range(chunks):

        @pl.when(outer)
        def _():
            final_copy(k).wait_recv()

        stores.append(
            pltpu.make_async_copy(final_terms.at[k], kernel_out.at[:, pl.ds(k * width, width)], store_sem.at[k])
        )
        stores[-1].start()

    for h in range(PARTS):
        line_peers(lambda source, h=h: first_copy(h, source, z).wait_recv())
        total = jnp.sum(first_terms[h].astype(F32), axis=0) * factor_share
        first_out[:, h] = total.reshape(n, part, rows)

    for store in stores:
        store.wait()
    for k in range(chunks):
        peers(lambda target, k=k: out_copy(k, me, target).wait_send())
        peers(lambda target, k=k: back_copy(k, me, target).wait_send())

        @pl.when(outer)
        def _():
            outer_copy(k).wait_send()

        @pl.when(inner)
        def _():
            pair_copy(k).wait_send()
            final_copy(k).wait_send()

    line_peers(lambda target: second_copy(z, target).wait_send())
    for h in range(1, PARTS):
        peers(lambda target, h=h: late_copy(h, me, target).wait_send())
    for h in range(PARTS):
        line_peers(lambda target, h=h: first_copy(h, z, target).wait_send())


def fused(n, groups, tokens, cotangent, kernel, first_factor, second_factor):
    rows, channels = tokens.shape[1:]
    chunks = CHUNKS
    width = channels // chunks
    block = rows // n
    part = block // PARTS
    seq_share = 1.0 / math.sqrt(groups)
    factor_share = 1.0 / math.sqrt(2.0 * channels * groups)
    second = jnp.transpose(second_factor, (1, 2, 0))
    any_spec = pl.BlockSpec(memory_space=pl.ANY)
    vmem_spec = pl.BlockSpec(memory_space=pltpu.VMEM)
    dma = pltpu.SemaphoreType.DMA
    kernel_grad, first_grad, second_grad = pl.pallas_call(
        functools.partial(mixer_kernel, n, groups, chunks, seq_share, factor_share),
        out_shape=(
            jax.ShapeDtypeStruct((rows, channels), BF16),
            jax.ShapeDtypeStruct((n, PARTS, part, rows), F32),
            jax.ShapeDtypeStruct((n, n, block), F32),
        ),
        in_specs=[any_spec] * 4 + [vmem_spec],
        out_specs=(any_spec, vmem_spec, vmem_spec),
        scratch_shapes=[
            pltpu.VMEM((rows, rows), BF16),
            pltpu.VMEM((chunks, rows, width), BF16),
            pltpu.VMEM((chunks, rows, width), BF16),
            pltpu.VMEM((chunks, rows, width), BF16),
            pltpu.VMEM((rows, rows), BF16),
            pltpu.VMEM((rows, rows), BF16),
            pltpu.VMEM((chunks, n, 2, block, width), BF16),
            pltpu.VMEM((chunks, n, 2, block, width), BF16),
            pltpu.VMEM((PARTS, n, chunks, 2 * part, width), BF16),
            pltpu.VMEM((PARTS, n, chunks, 2 * part, width), BF16),
            pltpu.VMEM((chunks, rows, width), F32),
            pltpu.VMEM((chunks, rows, width), BF16),
            pltpu.VMEM((chunks, rows, width), BF16),
            pltpu.VMEM((chunks, rows, width), BF16),
            pltpu.VMEM((chunks, rows, width), BF16),
            pltpu.VMEM((rows, rows), F32),
            pltpu.VMEM((groups, n, rows), F32),
            pltpu.VMEM((n, part, rows), F32),
            pltpu.VMEM((PARTS, groups, n * part, rows), BF16),
            dma((chunks, 3)),
            dma,
            dma((chunks,)),
            dma((chunks, n)),
            dma((chunks, n)),
            dma((chunks, n)),
            dma((chunks, n)),
            dma((PARTS, n)),
            dma((PARTS, n)),
            dma((chunks,)),
            dma((chunks,)),
            dma((chunks,)),
            dma((chunks,)),
            dma((chunks,)),
            dma((chunks,)),
            dma((groups,)),
            dma((groups,)),
            dma((PARTS, groups)),
            dma((PARTS, groups)),
        ],
        compiler_params=pltpu.CompilerParams(
            collective_id=0, has_side_effects=True, vmem_limit_bytes=60 * 1024 * 1024
        ),
        cost_estimate=pl.CostEstimate(
            flops=16 * rows * rows * channels, bytes_accessed=8 * rows * channels, transcendentals=0
        ),
    )(tokens, cotangent, kernel, first_factor, second)
    second_grad = jnp.transpose(second_grad, (2, 0, 1))
    return kernel_grad, first_grad.reshape(1, rows, rows), second_grad


def separate(tokens, cotangent, kernel, first_factor, second_factor):
    local_rows = tokens.shape[1]
    channels = tokens.shape[2]
    column_blocks = second_factor.shape[0]
    mixed_in = jnp.einsum(
        "aqb,abc->aqc", first_factor, tokens, preferred_element_type=jnp.float32
    ).astype(jnp.bfloat16)
    mixed_up = jnp.einsum(
        "aqb,abc->aqc", first_factor, cotangent, preferred_element_type=jnp.float32
    ).astype(jnp.bfloat16)
    arrived_in = lax.all_to_all(mixed_in, "seq", split_axis=1, concat_axis=0, tiled=True)
    arrived_up = lax.all_to_all(mixed_up, "seq", split_axis=1, concat_axis=0, tiled=True)
    forward = jnp.einsum(
        "bpa,abc->bpc", second_factor, arrived_in, preferred_element_type=jnp.float32
    )
    backward = jnp.einsum(
        "bpa,abc->bpc", second_factor, arrived_up, preferred_element_type=jnp.float32
    )
    arrived_in, arrived_up, forward, backward = (arrived_in, arrived_up, forward, backward)
    kernel_local = kernel.reshape(column_blocks, -1, channels)
    kernel_grad = forward * backward
    weighted = (kernel_local * forward).astype(jnp.bfloat16)
    pulled = (kernel_local * backward).astype(jnp.bfloat16)
    second_grad = jnp.einsum(
        "bpc,abc->bpa", pulled, arrived_in, preferred_element_type=jnp.float32
    ) + jnp.einsum("bpc,abc->bpa", weighted, arrived_up, preferred_element_type=jnp.float32)
    spread = jnp.einsum(
        "bpa,bpc->abc", second_factor, weighted, preferred_element_type=jnp.float32
    ).astype(jnp.bfloat16)
    pulled_back = jnp.einsum(
        "bpa,bpc->abc", second_factor, pulled, preferred_element_type=jnp.float32
    ).astype(jnp.bfloat16)
    seq_share = 1.0 / math.sqrt(lax.axis_size("dp"))
    factor_share = 1.0 / math.sqrt(2.0 * channels * lax.axis_size("dp"))
    returned, returned_back = (
        lax.all_to_all(spread, "seq", split_axis=0, concat_axis=1, tiled=True),
        lax.all_to_all(pulled_back, "seq", split_axis=0, concat_axis=1, tiled=True),
    )
    first_grad = jnp.einsum(
        "aqc,abc->aqb", returned_back, tokens, preferred_element_type=jnp.float32
    ) + jnp.einsum("aqc,abc->aqb", returned, cotangent, preferred_element_type=jnp.float32)
    kernel_total, first_total, second_total = lax.psum((kernel_grad, first_grad, second_grad), "dp")
    kernel_out = (kernel_total * seq_share).astype(jnp.bfloat16)
    return (
        kernel_out.reshape(local_rows, channels),
        first_total * factor_share,
        second_total * factor_share,
    )


def shards(tokens, cotangent, kernel, first_factor, second_factor):
    n = lax.axis_size("seq")
    groups = lax.axis_size("dp")
    rows, channels = tokens.shape[1:]
    fits = (
        groups == 4
        and first_factor.shape[0] == 1
        and second_factor.shape[1] == n
        and second_factor.shape[0] == 8 * PARTS
        and n == 8
        and channels % (128 * CHUNKS) == 0
        and rows == n * second_factor.shape[0]
    )
    arguments = (tokens, cotangent, kernel, first_factor, second_factor)
    return fused(n, groups, *arguments) if fits else separate(*arguments)


def solution(mesh):
    in_specs = (
        P("dp", "seq", None),
        P("dp", "seq", None),
        P("seq", None),
        P("seq", None, None),
        P("seq", None, None),
    )
    out_specs = (P("seq", None), P("seq", None, None), P("seq", None, None))
    return jax.shard_map(shards, mesh=mesh, in_specs=in_specs, out_specs=out_specs, check_vma=False)
```

```python
import functools
import math

import jax
import jax.numpy as jnp
from jax import lax
from jax.experimental import pallas as pl
from jax.experimental.pallas import tpu as pltpu
from jax.sharding import PartitionSpec as P

MESH = pl.DeviceIdType.MESH
BF16 = jnp.bfloat16
F32 = jnp.float32
HALVES = 2
CHUNKS = 8
LAG = 4


def dot(left, right):
    return jnp.dot(left, right, preferred_element_type=F32)


def dot_rows(left, right):
    return lax.dot_general(left, right, (((1,), (1,)), ((), ())), preferred_element_type=F32)


def mixer_kernel(
    n,
    groups,
    chunks,
    seq_share,
    factor_share,
    tokens_ref,
    cotangent_ref,
    kernel_ref,
    first_ref,
    second_ref,
    kernel_out,
    first_out,
    second_out,
    first_v,
    tokens_v,
    cotangent_v,
    kernel_v,
    factor_v,
    factor_t_v,
    mixed,
    arrived,
    spread,
    returned,
    own_terms,
    outer_terms,
    pair_terms,
    other_terms,
    final_terms,
    second_acc,
    second_terms,
    first_acc,
    first_terms,
    load_sem,
    first_load_sem,
    store_sem,
    out_send,
    out_recv,
    back_send,
    back_recv,
    outer_send,
    outer_recv,
    pair_send,
    pair_recv,
    final_send,
    final_recv,
    second_send,
    second_recv,
    first_send,
    first_recv,
):
    me = lax.axis_index("seq")
    z = lax.axis_index("dp")
    inner = jnp.logical_and(z >= 1, z <= 2)
    outer = jnp.logical_not(inner)
    rows = first_v.shape[0]
    width = tokens_v.shape[2]
    block = rows // n
    part = block // HALVES

    first_load = pltpu.make_async_copy(first_ref.at[0], first_v, first_load_sem)
    first_load.start()
    loads = []
    for k in range(chunks):
        columns = pl.ds(k * width, width)
        trio = [
            pltpu.make_async_copy(tokens_ref.at[0, :, columns], tokens_v.at[k], load_sem.at[k, 0]),
            pltpu.make_async_copy(cotangent_ref.at[0, :, columns], cotangent_v.at[k], load_sem.at[k, 1]),
            pltpu.make_async_copy(kernel_ref.at[:, columns], kernel_v.at[k], load_sem.at[k, 2]),
        ]
        trio[0].start()
        trio[1].start()
        loads.append(trio)
    for trio in loads:
        trio[2].start()

    barrier = pltpu.get_barrier_semaphore()
    for d in range(1, n):
        pl.semaphore_signal(barrier, inc=1, device_id={"seq": lax.rem(me + d, n)}, device_id_type=MESH)
    for d in range(1, groups):
        pl.semaphore_signal(barrier, inc=1, device_id={"dp": lax.rem(z + d, groups)}, device_id_type=MESH)

    shape = (n, block, rows)
    row_block = lax.broadcasted_iota(jnp.int32, shape, 1) * n
    column = lax.broadcasted_iota(jnp.int32, shape, 2)
    same_block = jnp.logical_and(column >= row_block, column < row_block + n)
    pick_block = lax.broadcasted_iota(jnp.int32, (block, rows), 0) * n
    pick_column = lax.broadcasted_iota(jnp.int32, (block, rows), 1)
    picks = [(pick_column == pick_block + p).astype(F32).astype(BF16) for p in range(n)]
    second = sum(dot(second_ref[p], picks[p]) for p in range(n))
    spread_factor = jnp.broadcast_to(second[:, None, :], shape)
    transposed = jnp.where(same_block, spread_factor, 0.0).reshape(rows, rows)
    factor_t_v[...] = transposed.astype(BF16)
    factor_v[...] = transposed.T.astype(BF16)
    second_acc[...] = jnp.zeros_like(second_acc)

    def out_copy(k, source, target):
        return pltpu.make_async_remote_copy(
            src_ref=mixed.at[k, target],
            dst_ref=arrived.at[k, source],
            send_sem=out_send.at[k, target],
            recv_sem=out_recv.at[k, source],
            device_id={"seq": target},
            device_id_type=MESH,
        )

    def back_copy(h, k, source, target):
        return pltpu.make_async_remote_copy(
            src_ref=spread.at[h, k, target],
            dst_ref=returned.at[h, k, source],
            send_sem=back_send.at[h, k, target],
            recv_sem=back_recv.at[h, k, source],
            device_id={"seq": target},
            device_id_type=MESH,
        )

    def line_copy(src, dst, send, recv, target):
        return pltpu.make_async_remote_copy(
            src_ref=src,
            dst_ref=dst,
            send_sem=send,
            recv_sem=recv,
            device_id={"dp": target},
            device_id_type=MESH,
        )

    inner_partner = 1 + z // 3
    outer_partner = (z - 1) * 3
    other_inner = 3 - z

    def outer_copy(k):
        return line_copy(pair_terms.at[k], outer_terms.at[k], outer_send.at[k], outer_recv.at[k], inner_partner)

    def pair_copy(k):
        return line_copy(pair_terms.at[k], other_terms.at[k], pair_send.at[k], pair_recv.at[k], other_inner)

    def final_copy(k):
        return line_copy(final_terms.at[k], final_terms.at[k], final_send.at[k], final_recv.at[k], outer_partner)

    def second_copy(source, target):
        return line_copy(
            second_terms.at[source], second_terms.at[source], second_send.at[target], second_recv.at[source], target
        )

    def first_copy(h, source, target):
        return line_copy(
            first_terms.at[h, source], first_terms.at[h, source], first_send.at[h, target], first_recv.at[h, source], target
        )

    def peers(action):
        def step(d, carry):
            action(lax.rem(me + d, n))
            return carry

        lax.fori_loop(1, n, step, 0)

    def line_peers(action):
        for d in range(1, groups):
            action(lax.rem(z + d, groups))

    first_load.wait()
    for k in range(chunks):
        loads[k][0].wait()
        loads[k][1].wait()
        mixed[k, :, 0] = dot(first_v[...], tokens_v[k]).astype(BF16).reshape(n, block, width)
        mixed[k, :, 1] = dot(first_v[...], cotangent_v[k]).astype(BF16).reshape(n, block, width)
        if k == 0:
            pl.semaphore_wait(barrier, n + groups - 2)
        peers(lambda target, k=k: out_copy(k, me, target).start())
        arrived[k, me] = mixed[k, me]
    for trio in loads:
        trio[2].wait()

    def make_pair(k):
        outer_copy(k).wait_recv()
        pair_terms[k] = (own_terms[k] + outer_terms[k].astype(F32)).astype(BF16)
        pair_copy(k).start()

    def make_final(k):
        pair_copy(k).wait_recv()
        total = pair_terms[k].astype(F32) + other_terms[k].astype(F32)
        final_terms[k] = (total * seq_share).astype(BF16)
        final_copy(k).start()

    def transform(k, carry):
        peers(lambda source: out_copy(k, source, me).wait_recv())
        mixed_in = arrived[k, :, 0].reshape(rows, width)
        mixed_up = arrived[k, :, 1].reshape(rows, width)
        forward = dot(factor_v[...], mixed_in)
        backward = dot(factor_v[...], mixed_up)
        terms = forward * backward
        gains = kernel_v[k].astype(F32)
        weighted = (gains * forward).astype(BF16)
        pulled = (gains * backward).astype(BF16)
        back = dot(factor_t_v[...], pulled).astype(BF16).reshape(n, HALVES, part, width)
        ahead = dot(factor_t_v[...], weighted).astype(BF16).reshape(n, HALVES, part, width)
        for h in range(HALVES):
            spread[h, k, :, 0] = back[:, h]
            spread[h, k, :, 1] = ahead[:, h]
        peers(lambda target: back_copy(0, k, me, target).start())

        @pl.when(outer)
        def _():
            pair_terms[k] = terms.astype(BF16)
            outer_copy(k).start()

        @pl.when(inner)
        def _():
            own_terms[k] = terms

        for h in range(HALVES):
            returned[h, k, me] = spread[h, k, me]
        second_acc[...] += dot_rows(mixed_in, pulled) + dot_rows(mixed_up, weighted)

        @pl.when(jnp.logical_and(inner, k >= LAG))
        def _():
            make_pair(k - LAG)

        return carry

    lax.fori_loop(0, chunks, transform, 0)
    for h in range(1, HALVES):
        for k in range(chunks):
            peers(lambda target, h=h, k=k: back_copy(h, k, me, target).start())

    second_terms[z] = jnp.sum(
        jnp.where(same_block, second_acc[...].reshape(shape), 0.0), axis=1
    )
    line_peers(lambda target: second_copy(z, target).start())

    @pl.when(inner)
    def _():
        def follow(k, carry):
            make_pair(k + LAG)
            make_final(k)
            return carry

        lax.fori_loop(0, chunks - LAG, follow, 0)

    for h in range(HALVES):
        first_acc[...] = jnp.zeros_like(first_acc)

        def gather(k, carry, h=h):
            peers(lambda source: back_copy(h, k, source, me).wait_recv())
            back = returned[h, k, :, 0].reshape(n * part, width)
            ahead = returned[h, k, :, 1].reshape(n * part, width)
            first_acc[...] += dot_rows(back, tokens_v[k]) + dot_rows(ahead, cotangent_v[k])
            return carry

        lax.fori_loop(0, chunks, gather, 0)
        first_terms[h, z] = first_acc[...].astype(BF16)
        line_peers(lambda target, h=h: first_copy(h, z, target).start())

        @pl.when(inner)
        def _():
            def follow(k, carry):
                make_final(k)
                return carry

            last = chunks - 1
            lax.fori_loop(chunks - LAG if h == 0 else last, last if h == 0 else chunks, follow, 0)

        if h == 0:
            line_peers(lambda source: second_copy(source, z).wait_recv())
            rest = jnp.sum(second_terms[...], axis=0) * factor_share
            pieces = []
            for _ in range(3):
                pieces.append(rest.astype(BF16))
                rest = rest - pieces[-1].astype(F32)
            for p in range(n):
                second_out[p] = sum(dot_rows(piece, picks[p]) for piece in reversed(pieces))

    stores = []
    for k in range(chunks):

        @pl.when(outer)
        def _():
            final_copy(k).wait_recv()

        stores.append(
            pltpu.make_async_copy(final_terms.at[k], kernel_out.at[:, pl.ds(k * width, width)], store_sem.at[k])
        )
        stores[-1].start()

    for h in range(HALVES):
        line_peers(lambda source, h=h: first_copy(h, source, z).wait_recv())
        total = jnp.sum(first_terms[h].astype(F32), axis=0) * factor_share
        first_out[:, h] = total.reshape(n, part, rows)

    for store in stores:
        store.wait()
    for k in range(chunks):
        peers(lambda target, k=k: out_copy(k, me, target).wait_send())
        for h in range(HALVES):
            peers(lambda target, h=h, k=k: back_copy(h, k, me, target).wait_send())

        @pl.when(outer)
        def _():
            outer_copy(k).wait_send()

        @pl.when(inner)
        def _():
            pair_copy(k).wait_send()
            final_copy(k).wait_send()

    line_peers(lambda target: second_copy(z, target).wait_send())
    for h in range(HALVES):
        line_peers(lambda target, h=h: first_copy(h, z, target).wait_send())


def fused(n, groups, tokens, cotangent, kernel, first_factor, second_factor):
    rows, channels = tokens.shape[1:]
    chunks = CHUNKS
    width = channels // chunks
    block = rows // n
    part = block // HALVES
    seq_share = 1.0 / math.sqrt(groups)
    factor_share = 1.0 / math.sqrt(2.0 * channels * groups)
    second = jnp.transpose(second_factor, (1, 2, 0))
    any_spec = pl.BlockSpec(memory_space=pl.ANY)
    vmem_spec = pl.BlockSpec(memory_space=pltpu.VMEM)
    dma = pltpu.SemaphoreType.DMA
    kernel_grad, first_grad, second_grad = pl.pallas_call(
        functools.partial(mixer_kernel, n, groups, chunks, seq_share, factor_share),
        out_shape=(
            jax.ShapeDtypeStruct((rows, channels), BF16),
            jax.ShapeDtypeStruct((n, HALVES, part, rows), F32),
            jax.ShapeDtypeStruct((n, n, block), F32),
        ),
        in_specs=[any_spec] * 4 + [vmem_spec],
        out_specs=(any_spec, vmem_spec, vmem_spec),
        scratch_shapes=[
            pltpu.VMEM((rows, rows), BF16),
            pltpu.VMEM((chunks, rows, width), BF16),
            pltpu.VMEM((chunks, rows, width), BF16),
            pltpu.VMEM((chunks, rows, width), BF16),
            pltpu.VMEM((rows, rows), BF16),
            pltpu.VMEM((rows, rows), BF16),
            pltpu.VMEM((chunks, n, 2, block, width), BF16),
            pltpu.VMEM((chunks, n, 2, block, width), BF16),
            pltpu.VMEM((HALVES, chunks, n, 2, part, width), BF16),
            pltpu.VMEM((HALVES, chunks, n, 2, part, width), BF16),
            pltpu.VMEM((chunks, rows, width), F32),
            pltpu.VMEM((chunks, rows, width), BF16),
            pltpu.VMEM((chunks, rows, width), BF16),
            pltpu.VMEM((chunks, rows, width), BF16),
            pltpu.VMEM((chunks, rows, width), BF16),
            pltpu.VMEM((rows, rows), F32),
            pltpu.VMEM((groups, n, rows), F32),
            pltpu.VMEM((n * part, rows), F32),
            pltpu.VMEM((HALVES, groups, n * part, rows), BF16),
            dma((chunks, 3)),
            dma,
            dma((chunks,)),
            dma((chunks, n)),
            dma((chunks, n)),
            dma((HALVES, chunks, n)),
            dma((HALVES, chunks, n)),
            dma((chunks,)),
            dma((chunks,)),
            dma((chunks,)),
            dma((chunks,)),
            dma((chunks,)),
            dma((chunks,)),
            dma((groups,)),
            dma((groups,)),
            dma((HALVES, groups)),
            dma((HALVES, groups)),
        ],
        compiler_params=pltpu.CompilerParams(
            collective_id=0, has_side_effects=True, vmem_limit_bytes=60 * 1024 * 1024
        ),
        cost_estimate=pl.CostEstimate(
            flops=16 * rows * rows * channels, bytes_accessed=8 * rows * channels, transcendentals=0
        ),
    )(tokens, cotangent, kernel, first_factor, second)
    second_grad = jnp.transpose(second_grad, (2, 0, 1))
    return kernel_grad, first_grad.reshape(1, rows, rows), second_grad


def separate(tokens, cotangent, kernel, first_factor, second_factor):
    local_rows = tokens.shape[1]
    channels = tokens.shape[2]
    column_blocks = second_factor.shape[0]
    mixed_in = jnp.einsum(
        "aqb,abc->aqc", first_factor, tokens, preferred_element_type=jnp.float32
    ).astype(jnp.bfloat16)
    mixed_up = jnp.einsum(
        "aqb,abc->aqc", first_factor, cotangent, preferred_element_type=jnp.float32
    ).astype(jnp.bfloat16)
    arrived_in = lax.all_to_all(mixed_in, "seq", split_axis=1, concat_axis=0, tiled=True)
    arrived_up = lax.all_to_all(mixed_up, "seq", split_axis=1, concat_axis=0, tiled=True)
    forward = jnp.einsum(
        "bpa,abc->bpc", second_factor, arrived_in, preferred_element_type=jnp.float32
    )
    backward = jnp.einsum(
        "bpa,abc->bpc", second_factor, arrived_up, preferred_element_type=jnp.float32
    )
    arrived_in, arrived_up, forward, backward = (arrived_in, arrived_up, forward, backward)
    kernel_local = kernel.reshape(column_blocks, -1, channels)
    kernel_grad = forward * backward
    weighted = (kernel_local * forward).astype(jnp.bfloat16)
    pulled = (kernel_local * backward).astype(jnp.bfloat16)
    second_grad = jnp.einsum(
        "bpc,abc->bpa", pulled, arrived_in, preferred_element_type=jnp.float32
    ) + jnp.einsum("bpc,abc->bpa", weighted, arrived_up, preferred_element_type=jnp.float32)
    spread = jnp.einsum(
        "bpa,bpc->abc", second_factor, weighted, preferred_element_type=jnp.float32
    ).astype(jnp.bfloat16)
    pulled_back = jnp.einsum(
        "bpa,bpc->abc", second_factor, pulled, preferred_element_type=jnp.float32
    ).astype(jnp.bfloat16)
    seq_share = 1.0 / math.sqrt(lax.axis_size("dp"))
    factor_share = 1.0 / math.sqrt(2.0 * channels * lax.axis_size("dp"))
    returned, returned_back = (
        lax.all_to_all(spread, "seq", split_axis=0, concat_axis=1, tiled=True),
        lax.all_to_all(pulled_back, "seq", split_axis=0, concat_axis=1, tiled=True),
    )
    first_grad = jnp.einsum(
        "aqc,abc->aqb", returned_back, tokens, preferred_element_type=jnp.float32
    ) + jnp.einsum("aqc,abc->aqb", returned, cotangent, preferred_element_type=jnp.float32)
    kernel_total, first_total, second_total = lax.psum((kernel_grad, first_grad, second_grad), "dp")
    kernel_out = (kernel_total * seq_share).astype(jnp.bfloat16)
    return (
        kernel_out.reshape(local_rows, channels),
        first_total * factor_share,
        second_total * factor_share,
    )


def shards(tokens, cotangent, kernel, first_factor, second_factor):
    n = lax.axis_size("seq")
    groups = lax.axis_size("dp")
    rows, channels = tokens.shape[1:]
    fits = (
        groups == 4
        and first_factor.shape[0] == 1
        and second_factor.shape[1] == n
        and second_factor.shape[0] % (16 * HALVES) == 0
        and channels % (128 * CHUNKS) == 0
        and rows == n * second_factor.shape[0]
    )
    arguments = (tokens, cotangent, kernel, first_factor, second_factor)
    return fused(n, groups, *arguments) if fits else separate(*arguments)


def solution(mesh):
    in_specs = (
        P("dp", "seq", None),
        P("dp", "seq", None),
        P("seq", None),
        P("seq", None, None),
        P("seq", None, None),
    )
    out_specs = (P("seq", None), P("seq", None, None), P("seq", None, None))
    return jax.shard_map(shards, mesh=mesh, in_specs=in_specs, out_specs=out_specs, check_vma=False)
```

```python
import functools
import math

import jax
import jax.numpy as jnp
from jax import lax
from jax.experimental import pallas as pl
from jax.experimental.pallas import tpu as pltpu
from jax.sharding import PartitionSpec as P

MESH = pl.DeviceIdType.MESH
BF16 = jnp.bfloat16
F32 = jnp.float32
HALVES = 2
CHUNKS = 4


def dot(left, right):
    return jnp.dot(left, right, preferred_element_type=F32)


def dot_rows(left, right):
    return lax.dot_general(left, right, (((1,), (1,)), ((), ())), preferred_element_type=F32)


def mixer_kernel(
    n,
    groups,
    chunks,
    seq_share,
    factor_share,
    tokens_ref,
    cotangent_ref,
    kernel_ref,
    first_ref,
    second_ref,
    kernel_out,
    first_out,
    second_out,
    first_v,
    tokens_v,
    cotangent_v,
    kernel_v,
    factor_v,
    factor_t_v,
    mixed,
    arrived,
    spread,
    returned,
    own_terms,
    outer_terms,
    pair_terms,
    other_terms,
    final_terms,
    second_acc,
    second_terms,
    first_acc,
    first_terms,
    load_sem,
    first_load_sem,
    store_sem,
    out_send,
    out_recv,
    back_send,
    back_recv,
    outer_send,
    outer_recv,
    pair_send,
    pair_recv,
    final_send,
    final_recv,
    second_send,
    second_recv,
    first_send,
    first_recv,
):
    me = lax.axis_index("seq")
    z = lax.axis_index("dp")
    inner = jnp.logical_and(z >= 1, z <= 2)
    outer = jnp.logical_not(inner)
    rows = first_v.shape[0]
    width = tokens_v.shape[2]
    block = rows // n
    part = block // HALVES

    first_load = pltpu.make_async_copy(first_ref.at[0], first_v, first_load_sem)
    first_load.start()
    loads = []
    for k in range(chunks):
        columns = pl.ds(k * width, width)
        trio = [
            pltpu.make_async_copy(tokens_ref.at[0, :, columns], tokens_v.at[k], load_sem.at[k, 0]),
            pltpu.make_async_copy(cotangent_ref.at[0, :, columns], cotangent_v.at[k], load_sem.at[k, 1]),
            pltpu.make_async_copy(kernel_ref.at[:, columns], kernel_v.at[k], load_sem.at[k, 2]),
        ]
        trio[0].start()
        trio[1].start()
        loads.append(trio)
    for trio in loads:
        trio[2].start()

    barrier = pltpu.get_barrier_semaphore()
    for d in range(1, n):
        pl.semaphore_signal(barrier, inc=1, device_id={"seq": lax.rem(me + d, n)}, device_id_type=MESH)
    for d in range(1, groups):
        pl.semaphore_signal(barrier, inc=1, device_id={"dp": lax.rem(z + d, groups)}, device_id_type=MESH)

    shape = (n, block, rows)
    row_block = lax.broadcasted_iota(jnp.int32, shape, 1) * n
    column = lax.broadcasted_iota(jnp.int32, shape, 2)
    same_block = jnp.logical_and(column >= row_block, column < row_block + n)
    pick_block = lax.broadcasted_iota(jnp.int32, (block, rows), 0) * n
    pick_column = lax.broadcasted_iota(jnp.int32, (block, rows), 1)
    picks = [(pick_column == pick_block + p).astype(F32).astype(BF16) for p in range(n)]
    second = sum(dot(second_ref[p], picks[p]) for p in range(n))
    spread_factor = jnp.broadcast_to(second[:, None, :], shape)
    transposed = jnp.where(same_block, spread_factor, 0.0).reshape(rows, rows)
    factor_t_v[...] = transposed.astype(BF16)
    factor_v[...] = transposed.T.astype(BF16)
    second_acc[...] = jnp.zeros_like(second_acc)

    def out_copy(k, source, target):
        return pltpu.make_async_remote_copy(
            src_ref=mixed.at[k, target],
            dst_ref=arrived.at[k, source],
            send_sem=out_send.at[k, target],
            recv_sem=out_recv.at[k, source],
            device_id={"seq": target},
            device_id_type=MESH,
        )

    def back_copy(h, k, source, target):
        return pltpu.make_async_remote_copy(
            src_ref=spread.at[h, k, target],
            dst_ref=returned.at[h, k, source],
            send_sem=back_send.at[h, k, target],
            recv_sem=back_recv.at[h, k, source],
            device_id={"seq": target},
            device_id_type=MESH,
        )

    def line_copy(src, dst, send, recv, target):
        return pltpu.make_async_remote_copy(
            src_ref=src,
            dst_ref=dst,
            send_sem=send,
            recv_sem=recv,
            device_id={"dp": target},
            device_id_type=MESH,
        )

    inner_partner = 1 + z // 3
    outer_partner = (z - 1) * 3
    other_inner = 3 - z

    def outer_copy(k):
        return line_copy(pair_terms.at[k], outer_terms.at[k], outer_send.at[k], outer_recv.at[k], inner_partner)

    def pair_copy(k):
        return line_copy(pair_terms.at[k], other_terms.at[k], pair_send.at[k], pair_recv.at[k], other_inner)

    def final_copy(k):
        return line_copy(final_terms.at[k], final_terms.at[k], final_send.at[k], final_recv.at[k], outer_partner)

    def second_copy(source, target):
        return line_copy(
            second_terms.at[source], second_terms.at[source], second_send.at[target], second_recv.at[source], target
        )

    def first_copy(h, source, target):
        return line_copy(
            first_terms.at[h, source], first_terms.at[h, source], first_send.at[h, target], first_recv.at[h, source], target
        )

    def peers(action):
        def step(d, carry):
            action(lax.rem(me + d, n))
            return carry

        lax.fori_loop(1, n, step, 0)

    def line_peers(action):
        for d in range(1, groups):
            action(lax.rem(z + d, groups))

    first_load.wait()
    for k in range(chunks):
        loads[k][0].wait()
        loads[k][1].wait()
        mixed[k, :, 0] = dot(first_v[...], tokens_v[k]).astype(BF16).reshape(n, block, width)
        mixed[k, :, 1] = dot(first_v[...], cotangent_v[k]).astype(BF16).reshape(n, block, width)
        if k == 0:
            pl.semaphore_wait(barrier, n + groups - 2)
        peers(lambda target, k=k: out_copy(k, me, target).start())
        arrived[k, me] = mixed[k, me]
    for trio in loads:
        trio[2].wait()

    def make_pair(k):
        outer_copy(k).wait_recv()
        pair_terms[k] = (own_terms[k] + outer_terms[k].astype(F32)).astype(BF16)
        pair_copy(k).start()

    def make_final(k):
        pair_copy(k).wait_recv()
        total = pair_terms[k].astype(F32) + other_terms[k].astype(F32)
        final_terms[k] = (total * seq_share).astype(BF16)
        final_copy(k).start()

    def transform(k, carry):
        peers(lambda source: out_copy(k, source, me).wait_recv())
        mixed_in = arrived[k, :, 0].reshape(rows, width)
        mixed_up = arrived[k, :, 1].reshape(rows, width)
        forward = dot(factor_v[...], mixed_in)
        backward = dot(factor_v[...], mixed_up)
        terms = forward * backward
        gains = kernel_v[k].astype(F32)
        weighted = (gains * forward).astype(BF16)
        pulled = (gains * backward).astype(BF16)
        back = dot(factor_t_v[...], pulled).astype(BF16).reshape(n, HALVES, part, width)
        ahead = dot(factor_t_v[...], weighted).astype(BF16).reshape(n, HALVES, part, width)
        for h in range(HALVES):
            spread[h, k, :, 0] = back[:, h]
            spread[h, k, :, 1] = ahead[:, h]
        peers(lambda target: back_copy(0, k, me, target).start())

        @pl.when(outer)
        def _():
            pair_terms[k] = terms.astype(BF16)
            outer_copy(k).start()

        @pl.when(inner)
        def _():
            own_terms[k] = terms

        for h in range(HALVES):
            returned[h, k, me] = spread[h, k, me]
        second_acc[...] += dot_rows(mixed_in, pulled) + dot_rows(mixed_up, weighted)

        @pl.when(jnp.logical_and(inner, k >= 1))
        def _():
            make_pair(k - 1)

        @pl.when(jnp.logical_and(inner, k >= 2))
        def _():
            make_final(k - 2)

        return carry

    lax.fori_loop(0, chunks, transform, 0)
    for h in range(1, HALVES):
        for k in range(chunks):
            peers(lambda target, h=h, k=k: back_copy(h, k, me, target).start())

    second_terms[z] = jnp.sum(
        jnp.where(same_block, second_acc[...].reshape(shape), 0.0), axis=1
    )
    line_peers(lambda target: second_copy(z, target).start())

    @pl.when(inner)
    def _():
        make_pair(chunks - 1)
        if chunks >= 2:
            make_final(chunks - 2)

    for h in range(HALVES):
        first_acc[...] = jnp.zeros_like(first_acc)

        def gather(k, carry, h=h):
            peers(lambda source: back_copy(h, k, source, me).wait_recv())
            back = returned[h, k, :, 0].reshape(n * part, width)
            ahead = returned[h, k, :, 1].reshape(n * part, width)
            first_acc[...] += dot_rows(back, tokens_v[k]) + dot_rows(ahead, cotangent_v[k])
            return carry

        lax.fori_loop(0, chunks, gather, 0)
        first_terms[h, z] = first_acc[...].astype(BF16)
        line_peers(lambda target, h=h: first_copy(h, z, target).start())
        if h == 0:

            @pl.when(inner)
            def _():
                make_final(chunks - 1)

    line_peers(lambda source: second_copy(source, z).wait_recv())
    rest = jnp.sum(second_terms[...], axis=0) * factor_share
    pieces = []
    for _ in range(3):
        pieces.append(rest.astype(BF16))
        rest = rest - pieces[-1].astype(F32)
    for p in range(n):
        second_out[p] = sum(dot_rows(piece, picks[p]) for piece in reversed(pieces))

    stores = []
    for k in range(chunks):

        @pl.when(outer)
        def _():
            final_copy(k).wait_recv()

        stores.append(
            pltpu.make_async_copy(final_terms.at[k], kernel_out.at[:, pl.ds(k * width, width)], store_sem.at[k])
        )
        stores[-1].start()

    for h in range(HALVES):
        line_peers(lambda source, h=h: first_copy(h, source, z).wait_recv())
        total = jnp.sum(first_terms[h].astype(F32), axis=0) * factor_share
        first_out[:, h] = total.reshape(n, part, rows)

    for store in stores:
        store.wait()
    for k in range(chunks):
        peers(lambda target, k=k: out_copy(k, me, target).wait_send())
        for h in range(HALVES):
            peers(lambda target, h=h, k=k: back_copy(h, k, me, target).wait_send())

        @pl.when(outer)
        def _():
            outer_copy(k).wait_send()

        @pl.when(inner)
        def _():
            pair_copy(k).wait_send()
            final_copy(k).wait_send()

    line_peers(lambda target: second_copy(z, target).wait_send())
    for h in range(HALVES):
        line_peers(lambda target, h=h: first_copy(h, z, target).wait_send())


def fused(n, groups, tokens, cotangent, kernel, first_factor, second_factor):
    rows, channels = tokens.shape[1:]
    chunks = CHUNKS
    width = channels // chunks
    block = rows // n
    part = block // HALVES
    seq_share = 1.0 / math.sqrt(groups)
    factor_share = 1.0 / math.sqrt(2.0 * channels * groups)
    second = jnp.transpose(second_factor, (1, 2, 0))
    any_spec = pl.BlockSpec(memory_space=pl.ANY)
    vmem_spec = pl.BlockSpec(memory_space=pltpu.VMEM)
    dma = pltpu.SemaphoreType.DMA
    kernel_grad, first_grad, second_grad = pl.pallas_call(
        functools.partial(mixer_kernel, n, groups, chunks, seq_share, factor_share),
        out_shape=(
            jax.ShapeDtypeStruct((rows, channels), BF16),
            jax.ShapeDtypeStruct((n, HALVES, part, rows), F32),
            jax.ShapeDtypeStruct((n, n, block), F32),
        ),
        in_specs=[any_spec] * 4 + [vmem_spec],
        out_specs=(any_spec, vmem_spec, vmem_spec),
        scratch_shapes=[
            pltpu.VMEM((rows, rows), BF16),
            pltpu.VMEM((chunks, rows, width), BF16),
            pltpu.VMEM((chunks, rows, width), BF16),
            pltpu.VMEM((chunks, rows, width), BF16),
            pltpu.VMEM((rows, rows), BF16),
            pltpu.VMEM((rows, rows), BF16),
            pltpu.VMEM((chunks, n, 2, block, width), BF16),
            pltpu.VMEM((chunks, n, 2, block, width), BF16),
            pltpu.VMEM((HALVES, chunks, n, 2, part, width), BF16),
            pltpu.VMEM((HALVES, chunks, n, 2, part, width), BF16),
            pltpu.VMEM((chunks, rows, width), F32),
            pltpu.VMEM((chunks, rows, width), BF16),
            pltpu.VMEM((chunks, rows, width), BF16),
            pltpu.VMEM((chunks, rows, width), BF16),
            pltpu.VMEM((chunks, rows, width), BF16),
            pltpu.VMEM((rows, rows), F32),
            pltpu.VMEM((groups, n, rows), F32),
            pltpu.VMEM((n * part, rows), F32),
            pltpu.VMEM((HALVES, groups, n * part, rows), BF16),
            dma((chunks, 3)),
            dma,
            dma((chunks,)),
            dma((chunks, n)),
            dma((chunks, n)),
            dma((HALVES, chunks, n)),
            dma((HALVES, chunks, n)),
            dma((chunks,)),
            dma((chunks,)),
            dma((chunks,)),
            dma((chunks,)),
            dma((chunks,)),
            dma((chunks,)),
            dma((groups,)),
            dma((groups,)),
            dma((HALVES, groups)),
            dma((HALVES, groups)),
        ],
        compiler_params=pltpu.CompilerParams(
            collective_id=0, has_side_effects=True, vmem_limit_bytes=48 * 1024 * 1024
        ),
        cost_estimate=pl.CostEstimate(
            flops=16 * rows * rows * channels, bytes_accessed=8 * rows * channels, transcendentals=0
        ),
    )(tokens, cotangent, kernel, first_factor, second)
    second_grad = jnp.transpose(second_grad, (2, 0, 1))
    return kernel_grad, first_grad.reshape(1, rows, rows), second_grad


def separate(tokens, cotangent, kernel, first_factor, second_factor):
    local_rows = tokens.shape[1]
    channels = tokens.shape[2]
    column_blocks = second_factor.shape[0]
    mixed_in = jnp.einsum(
        "aqb,abc->aqc", first_factor, tokens, preferred_element_type=jnp.float32
    ).astype(jnp.bfloat16)
    mixed_up = jnp.einsum(
        "aqb,abc->aqc", first_factor, cotangent, preferred_element_type=jnp.float32
    ).astype(jnp.bfloat16)
    arrived_in = lax.all_to_all(mixed_in, "seq", split_axis=1, concat_axis=0, tiled=True)
    arrived_up = lax.all_to_all(mixed_up, "seq", split_axis=1, concat_axis=0, tiled=True)
    forward = jnp.einsum(
        "bpa,abc->bpc", second_factor, arrived_in, preferred_element_type=jnp.float32
    )
    backward = jnp.einsum(
        "bpa,abc->bpc", second_factor, arrived_up, preferred_element_type=jnp.float32
    )
    arrived_in, arrived_up, forward, backward = (arrived_in, arrived_up, forward, backward)
    kernel_local = kernel.reshape(column_blocks, -1, channels)
    kernel_grad = forward * backward
    weighted = (kernel_local * forward).astype(jnp.bfloat16)
    pulled = (kernel_local * backward).astype(jnp.bfloat16)
    second_grad = jnp.einsum(
        "bpc,abc->bpa", pulled, arrived_in, preferred_element_type=jnp.float32
    ) + jnp.einsum("bpc,abc->bpa", weighted, arrived_up, preferred_element_type=jnp.float32)
    spread = jnp.einsum(
        "bpa,bpc->abc", second_factor, weighted, preferred_element_type=jnp.float32
    ).astype(jnp.bfloat16)
    pulled_back = jnp.einsum(
        "bpa,bpc->abc", second_factor, pulled, preferred_element_type=jnp.float32
    ).astype(jnp.bfloat16)
    seq_share = 1.0 / math.sqrt(lax.axis_size("dp"))
    factor_share = 1.0 / math.sqrt(2.0 * channels * lax.axis_size("dp"))
    returned, returned_back = (
        lax.all_to_all(spread, "seq", split_axis=0, concat_axis=1, tiled=True),
        lax.all_to_all(pulled_back, "seq", split_axis=0, concat_axis=1, tiled=True),
    )
    first_grad = jnp.einsum(
        "aqc,abc->aqb", returned_back, tokens, preferred_element_type=jnp.float32
    ) + jnp.einsum("aqc,abc->aqb", returned, cotangent, preferred_element_type=jnp.float32)
    kernel_total, first_total, second_total = lax.psum((kernel_grad, first_grad, second_grad), "dp")
    kernel_out = (kernel_total * seq_share).astype(jnp.bfloat16)
    return (
        kernel_out.reshape(local_rows, channels),
        first_total * factor_share,
        second_total * factor_share,
    )


def shards(tokens, cotangent, kernel, first_factor, second_factor):
    n = lax.axis_size("seq")
    groups = lax.axis_size("dp")
    rows, channels = tokens.shape[1:]
    fits = (
        groups == 4
        and first_factor.shape[0] == 1
        and second_factor.shape[1] == n
        and second_factor.shape[0] % (16 * HALVES) == 0
        and channels % (128 * CHUNKS) == 0
        and rows == n * second_factor.shape[0]
    )
    arguments = (tokens, cotangent, kernel, first_factor, second_factor)
    return fused(n, groups, *arguments) if fits else separate(*arguments)


def solution(mesh):
    in_specs = (
        P("dp", "seq", None),
        P("dp", "seq", None),
        P("seq", None),
        P("seq", None, None),
        P("seq", None, None),
    )
    out_specs = (P("seq", None), P("seq", None, None), P("seq", None, None))
    return jax.shard_map(shards, mesh=mesh, in_specs=in_specs, out_specs=out_specs, check_vma=False)
```

```python
import functools
import math

import jax
import jax.numpy as jnp
from jax import lax
from jax.experimental import pallas as pl
from jax.experimental.pallas import tpu as pltpu
from jax.sharding import PartitionSpec as P

MESH = pl.DeviceIdType.MESH
BF16 = jnp.bfloat16
F32 = jnp.float32
HALVES = 2
CHUNKS = 4


def dot(left, right):
    return jnp.dot(left, right, preferred_element_type=F32)


def dot_rows(left, right):
    return lax.dot_general(left, right, (((1,), (1,)), ((), ())), preferred_element_type=F32)


def mixer_kernel(
    n,
    groups,
    chunks,
    seq_share,
    factor_share,
    tokens_ref,
    cotangent_ref,
    kernel_ref,
    first_ref,
    second_ref,
    kernel_out,
    first_out,
    second_out,
    first_v,
    tokens_v,
    cotangent_v,
    kernel_v,
    factor_v,
    factor_t_v,
    mixed,
    arrived,
    spread,
    returned,
    own_terms,
    outer_terms,
    pair_terms,
    other_terms,
    final_terms,
    second_acc,
    second_terms,
    first_acc,
    first_terms,
    load_sem,
    first_load_sem,
    store_sem,
    out_send,
    out_recv,
    back_send,
    back_recv,
    outer_send,
    outer_recv,
    pair_send,
    pair_recv,
    final_send,
    final_recv,
    second_send,
    second_recv,
    first_send,
    first_recv,
):
    me = lax.axis_index("seq")
    z = lax.axis_index("dp")
    inner = jnp.logical_and(z >= 1, z <= 2)
    outer = jnp.logical_not(inner)
    rows = first_v.shape[0]
    width = tokens_v.shape[2]
    block = rows // n
    part = block // HALVES

    first_load = pltpu.make_async_copy(first_ref.at[0], first_v, first_load_sem)
    first_load.start()
    loads = []
    for k in range(chunks):
        columns = pl.ds(k * width, width)
        trio = [
            pltpu.make_async_copy(tokens_ref.at[0, :, columns], tokens_v.at[k], load_sem.at[k, 0]),
            pltpu.make_async_copy(cotangent_ref.at[0, :, columns], cotangent_v.at[k], load_sem.at[k, 1]),
            pltpu.make_async_copy(kernel_ref.at[:, columns], kernel_v.at[k], load_sem.at[k, 2]),
        ]
        trio[0].start()
        trio[1].start()
        loads.append(trio)
    for trio in loads:
        trio[2].start()

    barrier = pltpu.get_barrier_semaphore()
    for d in range(1, n):
        pl.semaphore_signal(barrier, inc=1, device_id={"seq": lax.rem(me + d, n)}, device_id_type=MESH)
    for d in range(1, groups):
        pl.semaphore_signal(barrier, inc=1, device_id={"dp": lax.rem(z + d, groups)}, device_id_type=MESH)

    shape = (n, block, rows)
    row_block = lax.broadcasted_iota(jnp.int32, shape, 1) * n
    column = lax.broadcasted_iota(jnp.int32, shape, 2)
    same_block = jnp.logical_and(column >= row_block, column < row_block + n)
    pick_block = lax.broadcasted_iota(jnp.int32, (block, rows), 0) * n
    pick_column = lax.broadcasted_iota(jnp.int32, (block, rows), 1)
    picks = [(pick_column == pick_block + p).astype(F32).astype(BF16) for p in range(n)]
    second = sum(dot(second_ref[p], picks[p]) for p in range(n))
    spread_factor = jnp.broadcast_to(second[:, None, :], shape)
    transposed = jnp.where(same_block, spread_factor, 0.0).reshape(rows, rows)
    factor_t_v[...] = transposed.astype(BF16)
    factor_v[...] = transposed.T.astype(BF16)
    second_acc[...] = jnp.zeros_like(second_acc)

    def out_copy(k, source, target):
        return pltpu.make_async_remote_copy(
            src_ref=mixed.at[k, target],
            dst_ref=arrived.at[k, source],
            send_sem=out_send.at[k, target],
            recv_sem=out_recv.at[k, source],
            device_id={"seq": target},
            device_id_type=MESH,
        )

    def back_copy(h, k, source, target):
        return pltpu.make_async_remote_copy(
            src_ref=spread.at[h, k, target],
            dst_ref=returned.at[h, k, source],
            send_sem=back_send.at[h, k, target],
            recv_sem=back_recv.at[h, k, source],
            device_id={"seq": target},
            device_id_type=MESH,
        )

    def line_copy(src, dst, send, recv, target):
        return pltpu.make_async_remote_copy(
            src_ref=src,
            dst_ref=dst,
            send_sem=send,
            recv_sem=recv,
            device_id={"dp": target},
            device_id_type=MESH,
        )

    inner_partner = 1 + z // 3
    outer_partner = (z - 1) * 3
    other_inner = 3 - z

    def outer_copy(k):
        return line_copy(pair_terms.at[k], outer_terms.at[k], outer_send.at[k], outer_recv.at[k], inner_partner)

    def pair_copy(k):
        return line_copy(pair_terms.at[k], other_terms.at[k], pair_send.at[k], pair_recv.at[k], other_inner)

    def final_copy(k):
        return line_copy(final_terms.at[k], final_terms.at[k], final_send.at[k], final_recv.at[k], outer_partner)

    def second_copy(source, target):
        return line_copy(
            second_terms.at[source], second_terms.at[source], second_send.at[target], second_recv.at[source], target
        )

    def first_copy(h, source, target):
        return line_copy(
            first_terms.at[h, source], first_terms.at[h, source], first_send.at[h, target], first_recv.at[h, source], target
        )

    def peers(action):
        def step(d, carry):
            action(lax.rem(me + d, n))
            return carry

        lax.fori_loop(1, n, step, 0)

    def line_peers(action):
        for d in range(1, groups):
            action(lax.rem(z + d, groups))

    first_load.wait()
    for k in range(chunks):
        loads[k][0].wait()
        loads[k][1].wait()
        mixed[k, :, 0] = dot(first_v[...], tokens_v[k]).astype(BF16).reshape(n, block, width)
        mixed[k, :, 1] = dot(first_v[...], cotangent_v[k]).astype(BF16).reshape(n, block, width)
        if k == 0:
            pl.semaphore_wait(barrier, n + groups - 2)
        peers(lambda target, k=k: out_copy(k, me, target).start())
        arrived[k, me] = mixed[k, me]
    for trio in loads:
        trio[2].wait()

    def make_pair(k):
        outer_copy(k).wait_recv()
        pair_terms[k] = (own_terms[k] + outer_terms[k].astype(F32)).astype(BF16)
        pair_copy(k).start()

    def make_final(k):
        pair_copy(k).wait_recv()
        total = pair_terms[k].astype(F32) + other_terms[k].astype(F32)
        final_terms[k] = (total * seq_share).astype(BF16)
        final_copy(k).start()

    def transform(k, carry):
        peers(lambda source: out_copy(k, source, me).wait_recv())
        mixed_in = arrived[k, :, 0].reshape(rows, width)
        mixed_up = arrived[k, :, 1].reshape(rows, width)
        forward = dot(factor_v[...], mixed_in)
        backward = dot(factor_v[...], mixed_up)
        terms = forward * backward
        gains = kernel_v[k].astype(F32)
        weighted = (gains * forward).astype(BF16)
        pulled = (gains * backward).astype(BF16)
        back = dot(factor_t_v[...], pulled).astype(BF16).reshape(n, HALVES, part, width)
        ahead = dot(factor_t_v[...], weighted).astype(BF16).reshape(n, HALVES, part, width)
        for h in range(HALVES):
            spread[h, k, :, 0] = back[:, h]
            spread[h, k, :, 1] = ahead[:, h]
        peers(lambda target: back_copy(0, k, me, target).start())

        @pl.when(outer)
        def _():
            pair_terms[k] = terms.astype(BF16)
            outer_copy(k).start()

        @pl.when(inner)
        def _():
            own_terms[k] = terms

        for h in range(HALVES):
            returned[h, k, me] = spread[h, k, me]
        second_acc[...] += dot_rows(mixed_in, pulled) + dot_rows(mixed_up, weighted)

        @pl.when(jnp.logical_and(inner, k >= 1))
        def _():
            make_pair(k - 1)

        @pl.when(jnp.logical_and(inner, k >= 2))
        def _():
            make_final(k - 2)

        return carry

    lax.fori_loop(0, chunks, transform, 0)
    for h in range(1, HALVES):
        for k in range(chunks):
            peers(lambda target, h=h, k=k: back_copy(h, k, me, target).start())

    second_terms[z] = jnp.sum(
        jnp.where(same_block, second_acc[...].reshape(shape), 0.0), axis=1
    )
    line_peers(lambda target: second_copy(z, target).start())

    @pl.when(inner)
    def _():
        make_pair(chunks - 1)
        if chunks >= 2:
            make_final(chunks - 2)

    for h in range(HALVES):
        first_acc[...] = jnp.zeros_like(first_acc)

        def gather(k, carry, h=h):
            peers(lambda source: back_copy(h, k, source, me).wait_recv())
            back = returned[h, k, :, 0].reshape(n * part, width)
            ahead = returned[h, k, :, 1].reshape(n * part, width)
            first_acc[...] += dot_rows(back, tokens_v[k]) + dot_rows(ahead, cotangent_v[k])
            return carry

        lax.fori_loop(0, chunks, gather, 0)
        first_terms[h, z] = first_acc[...].astype(BF16)
        line_peers(lambda target, h=h: first_copy(h, z, target).start())
        if h == 0:

            @pl.when(inner)
            def _():
                make_final(chunks - 1)

    line_peers(lambda source: second_copy(source, z).wait_recv())
    rest = jnp.sum(second_terms[...], axis=0) * factor_share
    pieces = []
    for _ in range(3):
        pieces.append(rest.astype(BF16))
        rest = rest - pieces[-1].astype(F32)
    for p in range(n):
        second_out[p] = sum(dot_rows(piece, picks[p]) for piece in reversed(pieces))

    stores = []
    for k in range(chunks):

        @pl.when(outer)
        def _():
            final_copy(k).wait_recv()

        stores.append(
            pltpu.make_async_copy(final_terms.at[k], kernel_out.at[:, pl.ds(k * width, width)], store_sem.at[k])
        )
        stores[-1].start()

    for h in range(HALVES):
        line_peers(lambda source, h=h: first_copy(h, source, z).wait_recv())
        total = jnp.sum(first_terms[h].astype(F32), axis=0) * factor_share
        first_out[:, h] = total.reshape(n, part, rows)

    for store in stores:
        store.wait()
    for k in range(chunks):
        peers(lambda target, k=k: out_copy(k, me, target).wait_send())
        for h in range(HALVES):
            peers(lambda target, h=h, k=k: back_copy(h, k, me, target).wait_send())

        @pl.when(outer)
        def _():
            outer_copy(k).wait_send()

        @pl.when(inner)
        def _():
            pair_copy(k).wait_send()
            final_copy(k).wait_send()

    line_peers(lambda target: second_copy(z, target).wait_send())
    for h in range(HALVES):
        line_peers(lambda target, h=h: first_copy(h, z, target).wait_send())


def fused(n, groups, tokens, cotangent, kernel, first_factor, second_factor):
    rows, channels = tokens.shape[1:]
    chunks = CHUNKS
    width = channels // chunks
    block = rows // n
    part = block // HALVES
    seq_share = 1.0 / math.sqrt(groups)
    factor_share = 1.0 / math.sqrt(2.0 * channels * groups)
    second = jnp.transpose(second_factor, (1, 2, 0))
    any_spec = pl.BlockSpec(memory_space=pl.ANY)
    vmem_spec = pl.BlockSpec(memory_space=pltpu.VMEM)
    dma = pltpu.SemaphoreType.DMA
    kernel_grad, first_grad, second_grad = pl.pallas_call(
        functools.partial(mixer_kernel, n, groups, chunks, seq_share, factor_share),
        out_shape=(
            jax.ShapeDtypeStruct((rows, channels), BF16),
            jax.ShapeDtypeStruct((n, HALVES, part, rows), F32),
            jax.ShapeDtypeStruct((n, n, block), F32),
        ),
        in_specs=[any_spec] * 4 + [vmem_spec],
        out_specs=(any_spec, vmem_spec, vmem_spec),
        scratch_shapes=[
            pltpu.VMEM((rows, rows), BF16),
            pltpu.VMEM((chunks, rows, width), BF16),
            pltpu.VMEM((chunks, rows, width), BF16),
            pltpu.VMEM((chunks, rows, width), BF16),
            pltpu.VMEM((rows, rows), BF16),
            pltpu.VMEM((rows, rows), BF16),
            pltpu.VMEM((chunks, n, 2, block, width), BF16),
            pltpu.VMEM((chunks, n, 2, block, width), BF16),
            pltpu.VMEM((HALVES, chunks, n, 2, part, width), BF16),
            pltpu.VMEM((HALVES, chunks, n, 2, part, width), BF16),
            pltpu.VMEM((chunks, rows, width), F32),
            pltpu.VMEM((chunks, rows, width), BF16),
            pltpu.VMEM((chunks, rows, width), BF16),
            pltpu.VMEM((chunks, rows, width), BF16),
            pltpu.VMEM((chunks, rows, width), BF16),
            pltpu.VMEM((rows, rows), F32),
            pltpu.VMEM((groups, n, rows), F32),
            pltpu.VMEM((n * part, rows), F32),
            pltpu.VMEM((HALVES, groups, n * part, rows), BF16),
            dma((chunks, 3)),
            dma,
            dma((chunks,)),
            dma((chunks, n)),
            dma((chunks, n)),
            dma((HALVES, chunks, n)),
            dma((HALVES, chunks, n)),
            dma((chunks,)),
            dma((chunks,)),
            dma((chunks,)),
            dma((chunks,)),
            dma((chunks,)),
            dma((chunks,)),
            dma((groups,)),
            dma((groups,)),
            dma((HALVES, groups)),
            dma((HALVES, groups)),
        ],
        compiler_params=pltpu.CompilerParams(
            collective_id=0, has_side_effects=True, vmem_limit_bytes=60 * 1024 * 1024
        ),
        cost_estimate=pl.CostEstimate(
            flops=16 * rows * rows * channels, bytes_accessed=8 * rows * channels, transcendentals=0
        ),
    )(tokens, cotangent, kernel, first_factor, second)
    second_grad = jnp.transpose(second_grad, (2, 0, 1))
    return kernel_grad, first_grad.reshape(1, rows, rows), second_grad


def separate(tokens, cotangent, kernel, first_factor, second_factor):
    local_rows = tokens.shape[1]
    channels = tokens.shape[2]
    column_blocks = second_factor.shape[0]
    mixed_in = jnp.einsum(
        "aqb,abc->aqc", first_factor, tokens, preferred_element_type=jnp.float32
    ).astype(jnp.bfloat16)
    mixed_up = jnp.einsum(
        "aqb,abc->aqc", first_factor, cotangent, preferred_element_type=jnp.float32
    ).astype(jnp.bfloat16)
    arrived_in = lax.all_to_all(mixed_in, "seq", split_axis=1, concat_axis=0, tiled=True)
    arrived_up = lax.all_to_all(mixed_up, "seq", split_axis=1, concat_axis=0, tiled=True)
    forward = jnp.einsum(
        "bpa,abc->bpc", second_factor, arrived_in, preferred_element_type=jnp.float32
    )
    backward = jnp.einsum(
        "bpa,abc->bpc", second_factor, arrived_up, preferred_element_type=jnp.float32
    )
    arrived_in, arrived_up, forward, backward = (arrived_in, arrived_up, forward, backward)
    kernel_local = kernel.reshape(column_blocks, -1, channels)
    kernel_grad = forward * backward
    weighted = (kernel_local * forward).astype(jnp.bfloat16)
    pulled = (kernel_local * backward).astype(jnp.bfloat16)
    second_grad = jnp.einsum(
        "bpc,abc->bpa", pulled, arrived_in, preferred_element_type=jnp.float32
    ) + jnp.einsum("bpc,abc->bpa", weighted, arrived_up, preferred_element_type=jnp.float32)
    spread = jnp.einsum(
        "bpa,bpc->abc", second_factor, weighted, preferred_element_type=jnp.float32
    ).astype(jnp.bfloat16)
    pulled_back = jnp.einsum(
        "bpa,bpc->abc", second_factor, pulled, preferred_element_type=jnp.float32
    ).astype(jnp.bfloat16)
    seq_share = 1.0 / math.sqrt(lax.axis_size("dp"))
    factor_share = 1.0 / math.sqrt(2.0 * channels * lax.axis_size("dp"))
    returned, returned_back = (
        lax.all_to_all(spread, "seq", split_axis=0, concat_axis=1, tiled=True),
        lax.all_to_all(pulled_back, "seq", split_axis=0, concat_axis=1, tiled=True),
    )
    first_grad = jnp.einsum(
        "aqc,abc->aqb", returned_back, tokens, preferred_element_type=jnp.float32
    ) + jnp.einsum("aqc,abc->aqb", returned, cotangent, preferred_element_type=jnp.float32)
    kernel_total, first_total, second_total = lax.psum((kernel_grad, first_grad, second_grad), "dp")
    kernel_out = (kernel_total * seq_share).astype(jnp.bfloat16)
    return (
        kernel_out.reshape(local_rows, channels),
        first_total * factor_share,
        second_total * factor_share,
    )


def shards(tokens, cotangent, kernel, first_factor, second_factor):
    n = lax.axis_size("seq")
    groups = lax.axis_size("dp")
    rows, channels = tokens.shape[1:]
    fits = (
        groups == 4
        and first_factor.shape[0] == 1
        and second_factor.shape[1] == n
        and second_factor.shape[0] % (16 * HALVES) == 0
        and channels % (128 * CHUNKS) == 0
        and rows == n * second_factor.shape[0]
    )
    arguments = (tokens, cotangent, kernel, first_factor, second_factor)
    return fused(n, groups, *arguments) if fits else separate(*arguments)


def solution(mesh):
    in_specs = (
        P("dp", "seq", None),
        P("dp", "seq", None),
        P("seq", None),
        P("seq", None, None),
        P("seq", None, None),
    )
    out_specs = (P("seq", None), P("seq", None, None), P("seq", None, None))
    return jax.shard_map(shards, mesh=mesh, in_specs=in_specs, out_specs=out_specs, check_vma=False)
```
